32 devices in a mesh: grp: 2 (over y), tile: 16 (over z, x, core).
Axes of the slice: x: 2, y: 2, z: 4, core: 2. Of those that a mesh axis runs over, the one named last changes fastest.
Arguments:
- level_set: float32 [640, 10240], P('grp', 'tile'), may hold values from -8 to 8
- fuel: int32 [640, 10240], P('grp', 'tile'), may hold values from 0 to 12
- wind: float32 [2, 32, 512], P(None, 'grp', 'tile'), may hold values from -6 to 6
- owner: int32 [2, 16], P('grp'), may hold values from 0 to 15, each once within a row
- active: int32 [4, 2, 16], P(None, 'grp', 'tile'), may hold values 0 or 1
- fuel_rate: float32 [13], replicated, may hold values from 0.05 to 0.3
- fuel_wind: float32 [13], replicated, may hold values from 0.01 to 0.05
- fuel_heat: float32 [13], replicated, may hold values from 0.5 to 4
Outputs:
- level_out: float32 [640, 10240], P('grp', 'tile')
- wind_out: float32 [2, 32, 512], P(None, 'grp', 'tile')
The draws below stay inside these ranges and needn't reach their ends.
Inputs may be any that keep to these rules, and one draw needn't show every extreme that they name: Each row of owner is a permutation of the 16 tiles of a group.
All inputs are finite; a program needn't handle non-finite values. No bound on the sum of `active` on one device may be relied on, other than what follows from the above.
Results may differ from the reference program's by a relative error of at most 0.0003.
Values sent between devices are 32-bit elements; how exact they have to be, the bound alone decides.
A program may use at most 64 MiB of HBM per device.

```python
import math
import jax
import jax.numpy as jnp

R = 20
NFUEL = 13
AY = 16
AX = 32
STEPS = 2
SUBSTEPS = 2
SUBS = 4
FY = 320
FX = 640
NAY = 32
NAX = 512
NFY = 640
NFX = 10240
N_GRP = 2
N_TILE = 16


def plant(values, rng, low, largest):
    index_at = [jax.random.randint(jax.random.fold_in(rng, axis), (), 0, length) for axis, length in enumerate(values.shape)]
    widest = values.shape.index(max(values.shape))
    neighbour = index_at[:widest] + [(index_at[widest] + 1) % values.shape[widest]] + index_at[widest + 1:]
    return values.at[tuple(index_at)].set(low).at[tuple(neighbour)].set(largest)


def block_levels(own_key, extent, split, smallest, high):
    gain, own = 1.0, jax.random.fold_in(own_key, 6)
    for position, shards_of in split:
        heights = jnp.exp(jax.random.uniform(jax.random.fold_in(own, position), (shards_of,), jnp.float32, smallest / len(split), high / len(split)))
        gain = gain * jnp.repeat(heights, extent[position] // shards_of).reshape([-1 if axis == position else 1 for axis in range(len(extent))])
    return gain


def gaussian(own_key, dims, deviation, most, split=(), dtype=jnp.bfloat16):
    entries = jax.random.normal(own_key, dims, jnp.float32) * deviation
    if len(split) > 0:
        entries = block_levels(own_key, dims, split, -0.22, 0.18) * entries
    return jnp.clip(entries, min=-most, max=most).astype(dtype)


def setup_inputs(seed: int = 0) -> dict:
    seeds = jax.random.split(jax.random.key(seed), 9)
    return {
        "level_set": gaussian(seeds[0], (NFY, NFX), 2.0, 8.0, ((0, 2), (1, 16)), jnp.float32),
        "fuel": plant(jax.random.randint(seeds[1], (NFY, NFX), 0, NFUEL), jax.random.fold_in(seeds[1], 1), 0, NFUEL - 1).astype(jnp.int32),
        "wind": gaussian(seeds[2], (2, NAY, NAX), 2.0, 6.0, ((1, 2), (2, 16)), jnp.float32),
        "owner": jax.vmap(lambda own: jax.random.permutation(own, N_TILE))(jax.random.split(seeds[3], N_GRP)).reshape((N_GRP, N_TILE)).astype(jnp.int32),
        "active": plant((jax.random.randint(seeds[4], (SUBS, N_GRP, N_TILE), 0, 3) < 2).astype(jnp.int32), jax.random.fold_in(seeds[4], 1), 0, 1),
        "fuel_rate": jnp.clip(jnp.exp(jax.random.uniform(seeds[5], (NFUEL,), jnp.float32, math.log(0.05), math.log(0.3))), 0.05, 0.3),
        "fuel_wind": jnp.clip(jnp.exp(jax.random.uniform(seeds[6], (NFUEL,), jnp.float32, math.log(0.01), math.log(0.05))), 0.01, 0.05),
        "fuel_heat": jnp.clip(jnp.exp(jax.random.uniform(seeds[7], (NFUEL,), jnp.float32, math.log(0.5), math.log(4.0))), 0.5, 4.0),
    }


def lookup(fuel, table):
    total = jnp.zeros(fuel.shape, jnp.float32)
    for category in range(NFUEL):
        total = total + jnp.where(fuel == category, table[category], jnp.float32(0.0))
    return total

def burnt(level):
    return 0.5 * (1.0 - jnp.tanh(level))

def reference(level_set, fuel, wind, owner, active, fuel_rate, fuel_wind, fuel_heat):
    groups = N_GRP
    tiles = N_TILE
    rate = lookup(fuel, fuel_rate)
    drift = lookup(fuel, fuel_wind)
    heat = lookup(fuel, fuel_heat)
    level = level_set
    inverse = jnp.argsort(owner, axis=1).astype(jnp.int32)
    counter = 0
    for atmos_step in range(STEPS):
        blocks = wind.reshape(2, groups, AY, tiles, AX)
        index = jnp.broadcast_to(owner[None, :, None, :, None], blocks.shape)
        readers = jnp.take_along_axis(blocks, index, axis=3).reshape(2, NAY, NAX)
        east = jnp.repeat(jnp.repeat(readers[0], R, axis=0), R, axis=1)
        north = jnp.repeat(jnp.repeat(readers[1], R, axis=0), R, axis=1)
        fine_flux = jnp.zeros(level.shape, jnp.float32)
        for substep in range(SUBSTEPS):
            padded = jnp.pad(level, 1, mode='edge')
            back_x = level - padded[1:-1, :-2]
            ahead_x = padded[1:-1, 2:] - level
            back_y = level - padded[:-2, 1:-1]
            ahead_y = padded[2:, 1:-1] - level
            slope = jnp.sqrt(jnp.maximum(back_x, 0.0) ** 2 + jnp.minimum(ahead_x, 0.0) ** 2 + jnp.maximum(back_y, 0.0) ** 2 + jnp.minimum(ahead_y, 0.0) ** 2 + 1e-12)
            carry = jnp.maximum(east, 0.0) * back_x + jnp.minimum(east, 0.0) * ahead_x + jnp.maximum(north, 0.0) * back_y + jnp.minimum(north, 0.0) * ahead_y
            candidate = level - rate * slope - drift * carry
            flags = active[counter] > 0
            gate = flags[:, None, :, None]
            newer = jnp.where(gate, candidate.reshape(groups, FY, tiles, FX), level.reshape(groups, FY, tiles, FX)).reshape(NFY, NFX)
            fine_flux = fine_flux + heat * (burnt(newer) - burnt(level))
            level = newer
            counter += 1
        coarse = fine_flux.reshape(NAY, R, NAX, R).sum(axis=(1, 3)) / float(R * R)
        coarse4 = coarse.reshape(groups, AY, tiles, AX)
        inv_index = jnp.broadcast_to(inverse[:, None, :, None], coarse4.shape)
        owned = jnp.take_along_axis(coarse4, inv_index, axis=2)
        padq = jnp.pad(owned, ((0, 0), (1, 1), (0, 0), (1, 1)), mode='edge')
        grad_x = (padq[:, 1:-1, :, 2:] - padq[:, 1:-1, :, :-2]) * 0.5
        grad_y = (padq[:, 2:, :, 1:-1] - padq[:, :-2, :, 1:-1]) * 0.5
        wind4 = wind.reshape(2, groups, AY, tiles, AX)
        new_east = 0.9 * wind4[0] + 40.0 * grad_x
        new_north = 0.9 * wind4[1] + 40.0 * grad_y
        wind = jnp.stack([new_east, new_north]).reshape(2, NAY, NAX)
    return (level, wind)
```

```python
import functools

import jax
import jax.numpy as jnp
from jax import lax
from jax.experimental import pallas as pl
from jax.experimental.pallas import tpu as pltpu
from jax.sharding import PartitionSpec as P

STEPS = 2
SUBSTEPS = 2
SUBS = STEPS * SUBSTEPS
MESH = pl.DeviceIdType.MESH
LANES = 128
ROWS = 8
F32 = jnp.float32
BF16 = jnp.bfloat16


def thirds(x):
    high = x.astype(BF16)
    rest = x - high.astype(F32)
    middle = rest.astype(BF16)
    low = (rest - middle.astype(F32)).astype(BF16)
    return [high, middle, low]


def exact_dots(arrays, right):
    pieces = [piece for x in arrays for piece in thirds(x)]
    full = jnp.dot(jnp.concatenate(pieces, axis=0), right, preferred_element_type=F32)
    m = arrays[0].shape[0]
    return [
        full[3 * i * m : (3 * i + 1) * m] + full[(3 * i + 1) * m : (3 * i + 2) * m] + full[(3 * i + 2) * m : (3 * i + 3) * m]
        for i in range(len(arrays))
    ]


def kernel(
    grps, tiles, atm_rows, atm_cols,
    level_ref, fuel_ref, wind_ref, owner_ref, active_ref, rate_tab, wind_tab, heat_tab,
    level_out, wind_out,
    lev_a, lev_b, fuel, rate, drift, heat, burn, row_sums, gust, spread, gather_cols,
    send, halo, wind_first, wind_last, slots_first, slots_last,
    load_sem, send_sem, recv_sem, wind_sem, out_sem,
):
    cell_rows, cell_cols = fuel.shape
    refine = cell_rows // atm_rows
    cols = cell_cols // LANES
    group = 2 * refine
    tiles_in = group // ROWS
    groups = cell_rows // group
    g, t = lax.axis_index("grp"), lax.axis_index("tile")

    load_level = [
        pltpu.make_async_copy(
            level_ref.at[:, pl.ds(c * LANES, LANES)], lev_a.at[c, pl.ds(ROWS, cell_rows), :], load_sem.at[c]
        )
        for c in range(cols)
    ]
    load_fuel = pltpu.make_async_copy(fuel_ref, fuel, load_sem.at[cols])
    outer, inner = (0, cols - 1), tuple(range(1, cols - 1))
    for c in outer + inner:
        load_level[c].start()
    load_fuel.start()

    barrier = pltpu.get_barrier_semaphore()
    for d in range(1, tiles):
        pl.semaphore_signal(barrier, inc=1, device_id=(g, lax.rem(t + d, tiles)), device_id_type=MESH)

    @pl.when(g > 0)
    def _():
        pl.semaphore_signal(barrier, inc=1, device_id=(g - 1, t), device_id_type=MESH)

    @pl.when(g < grps - 1)
    def _():
        pl.semaphore_signal(barrier, inc=1, device_id=(g + 1, t), device_id_type=MESH)

    lane = lax.broadcasted_iota(jnp.int32, (ROWS, LANES), 1)
    sub = lax.broadcasted_iota(jnp.int32, (ROWS, LANES), 0)
    lane16 = lax.broadcasted_iota(jnp.int32, (atm_rows, LANES), 1)
    sub16 = lax.broadcasted_iota(jnp.int32, (atm_rows, LANES), 0)
    quarter = atm_cols

    def pack(east, north):
        top, low = slice(0, ROWS), slice(ROWS, 2 * ROWS)
        return jnp.where(
            lane < quarter, east[top],
            jnp.where(
                lane < 2 * quarter, pltpu.roll(east[low], quarter, 1),
                jnp.where(lane < 3 * quarter, pltpu.roll(north[top], 2 * quarter, 1), pltpu.roll(north[low], 3 * quarter, 1)),
            ),
        )

    def unpack(packed):
        east = jnp.concatenate([packed, pltpu.roll(packed, 3 * quarter, 1)], axis=0)
        north = jnp.concatenate([pltpu.roll(packed, 2 * quarter, 1), pltpu.roll(packed, quarter, 1)], axis=0)
        return east, north

    def share(packed, source, slots, index):
        source[...] = packed
        slots[t] = packed
        for d in range(1, tiles):
            pltpu.make_async_remote_copy(
                src_ref=source, dst_ref=slots.at[t],
                send_sem=wind_sem.at[2 * index], recv_sem=wind_sem.at[2 * index + 1],
                device_id=(g, lax.rem(t + d, tiles)), device_id_type=MESH,
            ).start()

    def await_all(slots, sem):
        others = slots.at[pl.ds(0, tiles - 1)]
        pltpu.make_async_copy(others, others, sem).wait()

    def halo_copy(k, side, there):
        return pltpu.make_async_remote_copy(
            src_ref=send.at[k, side], dst_ref=halo.at[k, side],
            send_sem=send_sem.at[k, side], recv_sem=recv_sem.at[k, side],
            device_id=there, device_id_type=MESH,
        )

    going = (t < tiles - 1, t > 0, g < grps - 1, g > 0)
    coming = (t > 0, t < tiles - 1, g > 0, g < grps - 1)
    targets = ((g, t + 1), (g, t - 1), (g + 1, t), (g - 1, t))

    def start_sides(k, sides):
        for side in sides:
            @pl.when(going[side])
            def _(side=side):
                halo_copy(k, side, targets[side]).start()

            @pl.when(jnp.logical_not(coming[side]))
            def _(side=side):
                halo[k, side] = send[k, side ^ 1]

    def wait_sides(k):
        for side in range(4):
            @pl.when(coming[side])
            def _(side=side):
                halo_copy(k, side, targets[side ^ 1]).wait_recv()

    def start_columns(k, west_col, east_col):
        send[k, 1] = west_col
        send[k, 0] = east_col
        start_sides(k, (0, 1))

    def start_rows(k, level):
        for side, row in ((2, ROWS + cell_rows - 1), (3, ROWS)):
            send[k, side] = jnp.zeros((ROWS, LANES), F32)
            for c in range(cols):
                send[k, side, c : c + 1, :] = level[c, row : row + 1, :]
        start_sides(k, (2, 3))

    def place_rows(k, level):
        for side, row in ((2, ROWS - 1), (3, ROWS + cell_rows)):
            for c in range(cols):
                level[c, row : row + 1, :] = halo[k, side, c : c + 1, :]

    def columns_into(packs, k, first, last):
        west_pack, east_pack = packs
        west_pack = jnp.where(lane == k, pltpu.roll(first, k, 1), west_pack)
        east_pack = jnp.where(lane == k, pltpu.roll(last, k + 1, 1), east_pack)
        return west_pack, east_pack

    blank = jnp.zeros((atm_rows, LANES - atm_cols), F32)
    mine = [jnp.concatenate([wind_ref[i], blank], axis=1) for i in range(2)]
    packed_wind = pack(mine[0], mine[1])
    for c in outer:
        load_level[c].wait()

    def first_columns(i, packs):
        for q in range(tiles_in):
            k = i * tiles_in + q
            rows = pl.ds(pl.multiple_of(ROWS + k * ROWS, ROWS), ROWS)
            packs = columns_into(packs, k, lev_a[0, rows, :], lev_a[cols - 1, rows, :])
        return packs

    empty = jnp.zeros((ROWS, LANES), F32)
    packs = lax.fori_loop(0, groups, first_columns, (empty, empty))
    pl.semaphore_wait(barrier, tiles - 1 + (g > 0).astype(jnp.int32) + (g < grps - 1).astype(jnp.int32))
    share(packed_wind, wind_first, slots_first, 0)
    start_columns(0, *packs)
    for c in inner:
        load_level[c].wait()
    start_rows(0, lev_a)

    index = lax.broadcasted_iota(jnp.int32, spread.shape, 0) * refine
    place = lax.broadcasted_iota(jnp.int32, spread.shape, 1)
    spread[...] = jnp.where((place >= index) & (place < index + refine), 1.0, 0.0).astype(BF16)
    index = lax.broadcasted_iota(jnp.int32, gather_cols.shape, 1) * refine
    place = lax.broadcasted_iota(jnp.int32, gather_cols.shape, 0)
    gather_cols[...] = jnp.where((place >= index) & (place < index + refine), 1.0, 0.0).astype(BF16)

    def table(ref):
        values = jnp.zeros((ROWS, LANES), F32)
        for category in range(ref.shape[0]):
            values = jnp.where(lane == category, ref[category], values)
        return values

    tables = [table(ref) for ref in (rate_tab, wind_tab, heat_tab)]
    load_fuel.wait()

    def prepare(i, carry):
        for q in range(tiles_in):
            start = pl.multiple_of((i * tiles_in + q) * ROWS, ROWS)
            rows = pl.ds(start, ROWS)
            for c in range(cols):
                at = slice(c * LANES, (c + 1) * LANES)
                category = fuel[rows, at]
                for values, out in zip(tables, (rate, drift, heat)):
                    out[rows, at] = jnp.take_along_axis(values, category, axis=1, mode="promise_in_bounds")
                burn[rows, at] = jnp.tanh(lev_a[c, pl.ds(pl.multiple_of(start + ROWS, ROWS), ROWS), :])
        return carry

    lax.fori_loop(0, groups, prepare, 0)

    def expand(east, north):
        wide = exact_dots([east, north], spread[...])
        for part in range(2):
            for c in range(cols):
                gust[part, c] = wide[part][:, c * LANES : (c + 1) * LANES]

    await_all(slots_first, wind_sem.at[1])
    east, north = unpack(slots_first[owner_ref[0, t]])
    expand(east, north)

    def block(i, k, src, dst, want, packs):
        flux = k % SUBSTEPS == SUBSTEPS - 1
        burning = jnp.where(active_ref[k, 0, 0] > 0, F32(1.0), F32(0.0))
        ends = 0 in want
        if ends:
            west_halo, east_halo = halo[k, 0], halo[k, 1]
        around = sorted({n for c in want for n in (c - 1, c, c + 1) if 0 <= n < cols})
        winds = {}
        for c in want:
            winds[c] = [
                [jnp.broadcast_to(gust[part, c, pl.ds(2 * i + a, 1), :], (ROWS, LANES)) for a in range(2)] for part in range(2)
            ]
        sums = {c: [None, None] for c in want}

        def add(c, a, x):
            sums[c][a] = x if sums[c][a] is None else sums[c][a] + x

        for q in range(tiles_in):
            kk = i * tiles_in + q
            start = pl.multiple_of(kk * ROWS, ROWS)
            rows, padded = pl.ds(start, ROWS), pl.ds(pl.multiple_of(start + ROWS, ROWS), ROWS)
            here = {c: src[c, padded, :] for c in around}
            right = {c: pltpu.roll(here[c], 1, 1) for c in around if c in want or c + 1 in want}
            left = {c: pltpu.roll(here[c], LANES - 1, 1) for c in around if c in want or c - 1 in want}
            if ends:
                right[-1] = pltpu.roll(west_halo, lax.rem(LANES - kk, LANES), 1)
                left[cols] = pltpu.roll(east_halo, LANES - 1 - kk, 1)
            low, high = (q * ROWS) // refine, (q * ROWS + ROWS - 1) // refine
            split = refine * high - q * ROWS
            new_edge = {}
            for c in want:
                at = slice(c * LANES, (c + 1) * LANES)
                level = here[c]
                above = src[c, pl.ds(start + ROWS - 1, ROWS), :]
                below = src[c, pl.ds(start + ROWS + 1, ROWS), :]
                back_x = level - jnp.where(lane == 0, right[c - 1], right[c])
                ahead_x = jnp.where(lane == LANES - 1, left[c + 1], left[c]) - level
                back_y = level - above
                ahead_y = below - level
                square = (
                    jnp.maximum(back_x, 0.0) ** 2 + jnp.minimum(ahead_x, 0.0) ** 2
                    + jnp.maximum(back_y, 0.0) ** 2 + jnp.minimum(ahead_y, 0.0) ** 2 + 1e-12
                )
                slope = square * lax.rsqrt(square)
                if low == high:
                    east_w, north_w = winds[c][0][low], winds[c][1][low]
                else:
                    east_w = jnp.where(sub < split, winds[c][0][low], winds[c][0][high])
                    north_w = jnp.where(sub < split, winds[c][1][low], winds[c][1][high])
                carry = east_w * jnp.where(east_w > 0.0, back_x, ahead_x) + north_w * jnp.where(north_w > 0.0, back_y, ahead_y)
                newer = level - burning * (rate[rows, at] * slope + drift[rows, at] * carry)
                dst[c, padded, :] = newer
                new_edge[c] = newer
                if flux:
                    now = jnp.tanh(newer)
                    released = heat[rows, at] * (burn[rows, at] - now)
                    if k < SUBS - 1:
                        burn[rows, at] = now
                    if low == high:
                        add(c, low, released)
                    else:
                        add(c, low, jnp.where(sub < split, released, 0.0))
                        add(c, high, jnp.where(sub < split, 0.0, released))
            if ends and k < SUBS - 1:
                packs = columns_into(packs, kk, new_edge[0], new_edge[cols - 1])
        if flux:
            for c in want:
                for a in range(2):
                    row_sums[c, pl.ds(2 * i + a, 1), :] = jnp.sum(sums[c][a], axis=0, keepdims=True)
        return packs

    buffers = (lev_a, lev_b)
    store_level = [
        pltpu.make_async_copy(
            buffers[SUBS % 2].at[c, pl.ds(ROWS, cell_rows), :], level_out.at[:, pl.ds(c * LANES, LANES)], out_sem.at[c]
        )
        for c in range(cols)
    ]
    for k in range(SUBS):
        src, dst = buffers[k % 2], buffers[(k + 1) % 2]
        wait_sides(k)
        place_rows(k, src)
        packs = lax.fori_loop(0, groups, lambda i, p: block(i, k, src, dst, outer, p), (empty, empty))
        if k < SUBS - 1:
            start_columns(k + 1, *packs)
        else:
            for c in outer:
                store_level[c].start()

        def middle(i, carry):
            block(i, k, src, dst, inner, None)
            return carry

        lax.fori_loop(0, 2, lambda n, carry: middle(n * (groups - 1), carry), 0)
        if k < SUBS - 1:
            start_rows(k + 1, dst)
        lax.fori_loop(1, groups - 1, middle, 0)
        if k == SUBS - 1:
            for c in inner:
                store_level[c].start()
        if k % SUBSTEPS == SUBSTEPS - 1:
            coarse = exact_dots([jnp.concatenate([row_sums[c] for c in range(cols)], axis=1)], gather_cols[...])[0] * F32(0.5 / (refine * refine))
            west = jnp.where(lane16 == 0, coarse, pltpu.roll(coarse, 1, 1))
            east_c = jnp.where(lane16 == atm_cols - 1, coarse, pltpu.roll(coarse, LANES - 1, 1))
            up = jnp.where(sub16 == 0, coarse, pltpu.roll(coarse, 1, 0))
            down = jnp.where(sub16 == atm_rows - 1, coarse, pltpu.roll(coarse, atm_rows - 1, 0))
            east = 0.9 * east + 40.0 * ((east_c - west) * 0.5)
            north = 0.9 * north + 40.0 * ((down - up) * 0.5)
            if k < SUBS - 1:
                expand(east, north)

    share(pack(east, north), wind_last, slots_last, 1)
    source = jnp.int32(0)
    for j in range(tiles):
        source = jnp.where(owner_ref[0, j] == t, jnp.int32(j), source)
    await_all(slots_last, wind_sem.at[3])
    east, north = unpack(slots_last[source])
    wind_out[0] = east[:, :atm_cols]
    wind_out[1] = north[:, :atm_cols]
    for copy in store_level:
        copy.wait()
    await_all(slots_first, wind_sem.at[0])
    await_all(slots_last, wind_sem.at[2])
    for k in range(SUBS):
        for side in range(4):
            @pl.when(going[side])
            def _(k=k, side=side):
                halo_copy(k, side, targets[side]).wait_send()


def shards(grps, tiles, level_set, fuel, wind, owner, active, fuel_rate, fuel_wind, fuel_heat):
    cell_rows, cell_cols = level_set.shape
    atm_rows, atm_cols = wind.shape[1], wind.shape[2]
    cells = pltpu.VMEM((cell_rows, cell_cols), F32)
    cols = cell_cols // LANES
    padded = pltpu.VMEM((cols, cell_rows + 2 * ROWS, LANES), F32)
    tile = (ROWS, LANES)
    vmem, smem = pl.BlockSpec(memory_space=pltpu.VMEM), pl.BlockSpec(memory_space=pltpu.SMEM)
    anywhere = pl.BlockSpec(memory_space=pl.ANY)
    return pl.pallas_call(
        functools.partial(kernel, grps, tiles, atm_rows, atm_cols),
        out_shape=(jax.ShapeDtypeStruct(level_set.shape, F32), jax.ShapeDtypeStruct(wind.shape, F32)),
        in_specs=[anywhere, anywhere, vmem, smem, smem, smem, smem, smem],
        out_specs=(anywhere, vmem),
        scratch_shapes=[
            padded, padded,
            pltpu.VMEM((cell_rows, cell_cols), jnp.int32),
            cells, cells, cells, cells,
            pltpu.VMEM((cols, atm_rows, LANES), F32),
            pltpu.VMEM((2, cols, atm_rows, LANES), F32),
            pltpu.VMEM((LANES, cell_cols), BF16),
            pltpu.VMEM((cell_cols, LANES), BF16),
            pltpu.VMEM((SUBS, 4) + tile, F32),
            pltpu.VMEM((SUBS, 4) + tile, F32),
            pltpu.VMEM(tile, F32),
            pltpu.VMEM(tile, F32),
            pltpu.VMEM((tiles,) + tile, F32),
            pltpu.VMEM((tiles,) + tile, F32),
            pltpu.SemaphoreType.DMA((cols + 1,)),
            pltpu.SemaphoreType.DMA((SUBS, 4)),
            pltpu.SemaphoreType.DMA((SUBS, 4)),
            pltpu.SemaphoreType.DMA((4,)),
            pltpu.SemaphoreType.DMA((cols,)),
        ],
        compiler_params=pltpu.CompilerParams(
            collective_id=0, has_side_effects=True, vmem_limit_bytes=32 * 1024 * 1024
        ),
    )(level_set, fuel, wind, owner, active, fuel_rate, fuel_wind, fuel_heat)


def solution(mesh):
    in_specs = (
        P("grp", "tile"),
        P("grp", "tile"),
        P(None, "grp", "tile"),
        P("grp", None),
        P(None, "grp", "tile"),
        P(),
        P(),
        P(),
    )
    out_specs = (P("grp", "tile"), P(None, "grp", "tile"))
    body = functools.partial(shards, mesh.shape["grp"], mesh.shape["tile"])
    return jax.shard_map(body, mesh=mesh, in_specs=in_specs, out_specs=out_specs, check_vma=False)
```

```python
import functools

import jax
import jax.numpy as jnp
from jax import lax
from jax.experimental import pallas as pl
from jax.experimental.pallas import tpu as pltpu
from jax.sharding import PartitionSpec as P

STEPS = 2
SUBSTEPS = 2
SUBS = STEPS * SUBSTEPS
MESH = pl.DeviceIdType.MESH
LANES = 128
ROWS = 8
F32 = jnp.float32
BF16 = jnp.bfloat16


def thirds(x):
    high = x.astype(BF16)
    rest = x - high.astype(F32)
    middle = rest.astype(BF16)
    low = (rest - middle.astype(F32)).astype(BF16)
    return [high, middle, low]


def exact_dots(arrays, right):
    pieces = [piece for x in arrays for piece in thirds(x)]
    full = jnp.dot(jnp.concatenate(pieces, axis=0), right, preferred_element_type=F32)
    m = arrays[0].shape[0]
    return [
        full[3 * i * m : (3 * i + 1) * m] + full[(3 * i + 1) * m : (3 * i + 2) * m] + full[(3 * i + 2) * m : (3 * i + 3) * m]
        for i in range(len(arrays))
    ]


def kernel(
    grps, tiles, atm_rows, atm_cols,
    level_ref, fuel_ref, wind_any, owner_any, active_any, rate_any, drift_any, heat_any,
    level_out, wind_out,
    lev_a, lev_b, fuel, rate, drift, heat, burn, row_sums, gust, spread, gather_cols,
    send, halo, wind_first, wind_last, slots_first, slots_last,
    wind_ref, owner_ref, active_ref, rate_tab, wind_tab, heat_tab,
    load_sem, small_sem, send_sem, recv_sem, wind_sem, out_sem,
):
    cell_rows, cell_cols = fuel.shape
    refine = cell_rows // atm_rows
    cols = cell_cols // LANES
    group = 2 * refine
    tiles_in = group // ROWS
    groups = cell_rows // group
    g, t = lax.axis_index("grp"), lax.axis_index("tile")

    load_level = [
        pltpu.make_async_copy(
            level_ref.at[:, pl.ds(c * LANES, LANES)], lev_a.at[c, pl.ds(ROWS, cell_rows), :], load_sem.at[c]
        )
        for c in range(cols)
    ]
    load_fuel = pltpu.make_async_copy(fuel_ref, fuel, load_sem.at[cols])
    outer, inner = (0, cols - 1), tuple(range(1, cols - 1))
    small = [
        pltpu.make_async_copy(source, target, small_sem.at[i])
        for i, (source, target) in enumerate((
            (wind_any, wind_ref), (owner_any, owner_ref), (active_any, active_ref),
            (rate_any, rate_tab), (drift_any, wind_tab), (heat_any, heat_tab),
        ))
    ]
    for copy in small:
        copy.start()
    for c in outer + inner:
        load_level[c].start()
    load_fuel.start()

    barrier = pltpu.get_barrier_semaphore()
    for d in range(1, tiles):
        pl.semaphore_signal(barrier, inc=1, device_id=(g, lax.rem(t + d, tiles)), device_id_type=MESH)

    @pl.when(g > 0)
    def _():
        pl.semaphore_signal(barrier, inc=1, device_id=(g - 1, t), device_id_type=MESH)

    @pl.when(g < grps - 1)
    def _():
        pl.semaphore_signal(barrier, inc=1, device_id=(g + 1, t), device_id_type=MESH)

    lane = lax.broadcasted_iota(jnp.int32, (ROWS, LANES), 1)
    sub = lax.broadcasted_iota(jnp.int32, (ROWS, LANES), 0)
    lane16 = lax.broadcasted_iota(jnp.int32, (atm_rows, LANES), 1)
    sub16 = lax.broadcasted_iota(jnp.int32, (atm_rows, LANES), 0)
    quarter = atm_cols

    def pack(east, north):
        top, low = slice(0, ROWS), slice(ROWS, 2 * ROWS)
        return jnp.where(
            lane < quarter, east[top],
            jnp.where(
                lane < 2 * quarter, pltpu.roll(east[low], quarter, 1),
                jnp.where(lane < 3 * quarter, pltpu.roll(north[top], 2 * quarter, 1), pltpu.roll(north[low], 3 * quarter, 1)),
            ),
        )

    def unpack(packed):
        east = jnp.concatenate([packed, pltpu.roll(packed, 3 * quarter, 1)], axis=0)
        north = jnp.concatenate([pltpu.roll(packed, 2 * quarter, 1), pltpu.roll(packed, quarter, 1)], axis=0)
        return east, north

    def share(packed, source, slots, index):
        source[...] = packed
        slots[t] = packed
        for d in range(1, tiles):
            pltpu.make_async_remote_copy(
                src_ref=source, dst_ref=slots.at[t],
                send_sem=wind_sem.at[2 * index], recv_sem=wind_sem.at[2 * index + 1],
                device_id=(g, lax.rem(t + d, tiles)), device_id_type=MESH,
            ).start()

    def await_all(slots, sem):
        others = slots.at[pl.ds(0, tiles - 1)]
        pltpu.make_async_copy(others, others, sem).wait()

    def halo_copy(k, side, there):
        return pltpu.make_async_remote_copy(
            src_ref=send.at[k, side], dst_ref=halo.at[k, side],
            send_sem=send_sem.at[k, side], recv_sem=recv_sem.at[k, side],
            device_id=there, device_id_type=MESH,
        )

    going = (t < tiles - 1, t > 0, g < grps - 1, g > 0)
    coming = (t > 0, t < tiles - 1, g > 0, g < grps - 1)
    targets = ((g, t + 1), (g, t - 1), (g + 1, t), (g - 1, t))

    def start_sides(k, sides):
        for side in sides:
            @pl.when(going[side])
            def _(side=side):
                halo_copy(k, side, targets[side]).start()

            @pl.when(jnp.logical_not(coming[side]))
            def _(side=side):
                halo[k, side] = send[k, side ^ 1]

    def wait_sides(k):
        for side in range(4):
            @pl.when(coming[side])
            def _(side=side):
                halo_copy(k, side, targets[side ^ 1]).wait_recv()

    def start_columns(k, west_col, east_col):
        send[k, 1] = west_col
        send[k, 0] = east_col
        start_sides(k, (0, 1))

    def start_rows(k, level):
        for side, row in ((2, ROWS + cell_rows - 1), (3, ROWS)):
            send[k, side] = jnp.zeros((ROWS, LANES), F32)
            for c in range(cols):
                send[k, side, c : c + 1, :] = level[c, row : row + 1, :]
        start_sides(k, (2, 3))

    def place_rows(k, level):
        for side, row in ((2, ROWS - 1), (3, ROWS + cell_rows)):
            for c in range(cols):
                level[c, row : row + 1, :] = halo[k, side, c : c + 1, :]

    def columns_into(packs, k, first, last):
        west_pack, east_pack = packs
        west_pack = jnp.where(lane == k, pltpu.roll(first, k, 1), west_pack)
        east_pack = jnp.where(lane == k, pltpu.roll(last, k + 1, 1), east_pack)
        return west_pack, east_pack

    index = lax.broadcasted_iota(jnp.int32, spread.shape, 0) * refine
    place = lax.broadcasted_iota(jnp.int32, spread.shape, 1)
    spread[...] = jnp.where((place >= index) & (place < index + refine), 1.0, 0.0).astype(BF16)
    index = lax.broadcasted_iota(jnp.int32, gather_cols.shape, 1) * refine
    place = lax.broadcasted_iota(jnp.int32, gather_cols.shape, 0)
    gather_cols[...] = jnp.where((place >= index) & (place < index + refine), 1.0, 0.0).astype(BF16)

    def table(ref):
        values = jnp.zeros((ROWS, LANES), F32)
        for category in range(ref.shape[0]):
            values = jnp.where(lane == category, ref[category], values)
        return values

    for copy in small:
        copy.wait()
    tables = [table(ref) for ref in (rate_tab, wind_tab, heat_tab)]
    blank = jnp.zeros((atm_rows, LANES - atm_cols), F32)
    mine = [jnp.concatenate([wind_ref[i], blank], axis=1) for i in range(2)]
    packed_wind = pack(mine[0], mine[1])

    pl.semaphore_wait(barrier, tiles - 1 + (g > 0).astype(jnp.int32) + (g < grps - 1).astype(jnp.int32))
    share(packed_wind, wind_first, slots_first, 0)
    empty = jnp.zeros((ROWS, LANES), F32)
    packs = (empty, empty)
    for c in outer:
        load_level[c].wait()
    for k in range(cell_rows // ROWS):
        rows = pl.ds(ROWS + k * ROWS, ROWS)
        packs = columns_into(packs, k, lev_a[0, rows, :], lev_a[cols - 1, rows, :])
    start_columns(0, *packs)
    for c in inner:
        load_level[c].wait()
    start_rows(0, lev_a)

    load_fuel.wait()

    def prepare(i, carry):
        for q in range(tiles_in):
            start = pl.multiple_of((i * tiles_in + q) * ROWS, ROWS)
            rows = pl.ds(start, ROWS)
            for c in range(cols):
                at = slice(c * LANES, (c + 1) * LANES)
                category = fuel[rows, at]
                for values, out in zip(tables, (rate, drift, heat)):
                    out[rows, at] = jnp.take_along_axis(values, category, axis=1, mode="promise_in_bounds")
                burn[rows, at] = jnp.tanh(lev_a[c, pl.ds(pl.multiple_of(start + ROWS, ROWS), ROWS), :])
        return carry

    lax.fori_loop(0, groups, prepare, 0, unroll=2)

    def expand(east, north):
        wide = exact_dots([east, north], spread[...])
        for part in range(2):
            for c in range(cols):
                gust[part, c] = wide[part][:, c * LANES : (c + 1) * LANES]

    await_all(slots_first, wind_sem.at[1])
    east, north = unpack(slots_first[owner_ref[0, t]])
    expand(east, north)

    def block(i, k, src, dst, want, packs):
        flux = k % SUBSTEPS == SUBSTEPS - 1
        burning = jnp.where(active_ref[k] > 0, F32(1.0), F32(0.0))
        ends = 0 in want
        if ends:
            west_halo, east_halo = halo[k, 0], halo[k, 1]
        around = sorted({n for c in want for n in (c - 1, c, c + 1) if 0 <= n < cols})
        winds = {}
        for c in want:
            winds[c] = [
                [jnp.broadcast_to(gust[part, c, pl.ds(2 * i + a, 1), :], (ROWS, LANES)) for a in range(2)] for part in range(2)
            ]
        sums = {c: [None, None] for c in want}

        def add(c, a, x):
            sums[c][a] = x if sums[c][a] is None else sums[c][a] + x

        for q in range(tiles_in):
            kk = i * tiles_in + q
            start = pl.multiple_of(kk * ROWS, ROWS)
            rows, padded = pl.ds(start, ROWS), pl.ds(pl.multiple_of(start + ROWS, ROWS), ROWS)
            here = {c: src[c, padded, :] for c in around}
            right = {c: pltpu.roll(here[c], 1, 1) for c in around if c in want or c + 1 in want}
            left = {c: pltpu.roll(here[c], LANES - 1, 1) for c in around if c in want or c - 1 in want}
            if ends:
                right[-1] = pltpu.roll(west_halo, lax.rem(LANES - kk, LANES), 1)
                left[cols] = pltpu.roll(east_halo, LANES - 1 - kk, 1)
            low, high = (q * ROWS) // refine, (q * ROWS + ROWS - 1) // refine
            split = refine * high - q * ROWS
            new_edge = {}
            for c in want:
                at = slice(c * LANES, (c + 1) * LANES)
                level = here[c]
                above = src[c, pl.ds(start + ROWS - 1, ROWS), :]
                below = src[c, pl.ds(start + ROWS + 1, ROWS), :]
                back_x = level - jnp.where(lane == 0, right[c - 1], right[c])
                ahead_x = jnp.where(lane == LANES - 1, left[c + 1], left[c]) - level
                back_y = level - above
                ahead_y = below - level
                square = (
                    jnp.maximum(back_x, 0.0) ** 2 + jnp.minimum(ahead_x, 0.0) ** 2
                    + jnp.maximum(back_y, 0.0) ** 2 + jnp.minimum(ahead_y, 0.0) ** 2 + 1e-12
                )
                slope = square * lax.rsqrt(square)
                if low == high:
                    east_w, north_w = winds[c][0][low], winds[c][1][low]
                else:
                    east_w = jnp.where(sub < split, winds[c][0][low], winds[c][0][high])
                    north_w = jnp.where(sub < split, winds[c][1][low], winds[c][1][high])
                carry = east_w * jnp.where(east_w > 0.0, back_x, ahead_x) + north_w * jnp.where(north_w > 0.0, back_y, ahead_y)
                newer = level - burning * (rate[rows, at] * slope + drift[rows, at] * carry)
                dst[c, padded, :] = newer
                new_edge[c] = newer
                if flux:
                    now = jnp.tanh(newer)
                    released = heat[rows, at] * (burn[rows, at] - now)
                    if k < SUBS - 1:
                        burn[rows, at] = now
                    if low == high:
                        add(c, low, released)
                    else:
                        add(c, low, jnp.where(sub < split, released, 0.0))
                        add(c, high, jnp.where(sub < split, 0.0, released))
            if ends and k < SUBS - 1:
                packs = columns_into(packs, kk, new_edge[0], new_edge[cols - 1])
        if flux:
            for c in want:
                for a in range(2):
                    row_sums[c, pl.ds(pl.multiple_of((2 * i + a) * ROWS, ROWS), ROWS), :] = sums[c][a]
        return packs

    def total_rows(c):
        parts = [row_sums[c, pl.ds(s, atm_rows, stride=ROWS), :] for s in range(ROWS)]
        while len(parts) > 1:
            parts = [one + two for one, two in zip(parts[::2], parts[1::2])]
        return parts[0]

    buffers = (lev_a, lev_b)
    store_level = [
        pltpu.make_async_copy(
            buffers[SUBS % 2].at[c, pl.ds(ROWS, cell_rows), :], level_out.at[:, pl.ds(c * LANES, LANES)], out_sem.at[c]
        )
        for c in range(cols)
    ]
    for k in range(SUBS):
        src, dst = buffers[k % 2], buffers[(k + 1) % 2]
        wait_sides(k)
        place_rows(k, src)
        packs = lax.fori_loop(0, groups, lambda i, p: block(i, k, src, dst, outer, p), (empty, empty), unroll=2)
        if k < SUBS - 1:
            start_columns(k + 1, *packs)
        else:
            for c in outer:
                store_level[c].start()

        def middle(i, carry):
            block(i, k, src, dst, inner, None)
            return carry

        lax.fori_loop(0, 2, lambda n, carry: middle(n * (groups - 1), carry), 0, unroll=2)
        if k < SUBS - 1:
            start_rows(k + 1, dst)
        lax.fori_loop(1, groups - 1, middle, 0, unroll=2)
        if k == SUBS - 1:
            for c in inner:
                store_level[c].start()
        if k % SUBSTEPS == SUBSTEPS - 1:
            coarse = exact_dots([jnp.concatenate([total_rows(c) for c in range(cols)], axis=1)], gather_cols[...])[0] * F32(0.5 / (refine * refine))
            west = jnp.where(lane16 == 0, coarse, pltpu.roll(coarse, 1, 1))
            east_c = jnp.where(lane16 == atm_cols - 1, coarse, pltpu.roll(coarse, LANES - 1, 1))
            up = jnp.where(sub16 == 0, coarse, pltpu.roll(coarse, 1, 0))
            down = jnp.where(sub16 == atm_rows - 1, coarse, pltpu.roll(coarse, atm_rows - 1, 0))
            east = 0.9 * east + 40.0 * ((east_c - west) * 0.5)
            north = 0.9 * north + 40.0 * ((down - up) * 0.5)
            if k < SUBS - 1:
                expand(east, north)

    share(pack(east, north), wind_last, slots_last, 1)
    source = jnp.int32(0)
    for j in range(tiles):
        source = jnp.where(owner_ref[0, j] == t, jnp.int32(j), source)
    await_all(slots_last, wind_sem.at[3])
    east, north = unpack(slots_last[source])
    wind_out[0] = east[:, :atm_cols]
    wind_out[1] = north[:, :atm_cols]
    for copy in store_level:
        copy.wait()
    await_all(slots_first, wind_sem.at[0])
    await_all(slots_last, wind_sem.at[2])
    for k in range(SUBS):
        for side in range(4):
            @pl.when(going[side])
            def _(k=k, side=side):
                halo_copy(k, side, targets[side]).wait_send()


def shards(grps, tiles, level_set, fuel, wind, owner, active, fuel_rate, fuel_wind, fuel_heat):
    cell_rows, cell_cols = level_set.shape
    atm_rows, atm_cols = wind.shape[1], wind.shape[2]
    cells = pltpu.VMEM((cell_rows, cell_cols), F32)
    cols = cell_cols // LANES
    padded = pltpu.VMEM((cols, cell_rows + 2 * ROWS, LANES), F32)
    tile = (ROWS, LANES)
    vmem = pl.BlockSpec(memory_space=pltpu.VMEM)
    anywhere = pl.BlockSpec(memory_space=pl.ANY)
    return pl.pallas_call(
        functools.partial(kernel, grps, tiles, atm_rows, atm_cols),
        out_shape=(jax.ShapeDtypeStruct(level_set.shape, F32), jax.ShapeDtypeStruct(wind.shape, F32)),
        in_specs=[anywhere] * 8,
        out_specs=(anywhere, vmem),
        scratch_shapes=[
            padded, padded,
            pltpu.VMEM((cell_rows, cell_cols), jnp.int32),
            cells, cells, cells, cells,
            pltpu.VMEM((cols, atm_rows * ROWS, LANES), F32),
            pltpu.VMEM((2, cols, atm_rows, LANES), F32),
            pltpu.VMEM((LANES, cell_cols), BF16),
            pltpu.VMEM((cell_cols, LANES), BF16),
            pltpu.VMEM((SUBS, 4) + tile, F32),
            pltpu.VMEM((SUBS, 4) + tile, F32),
            pltpu.VMEM(tile, F32),
            pltpu.VMEM(tile, F32),
            pltpu.VMEM((tiles,) + tile, F32),
            pltpu.VMEM((tiles,) + tile, F32),
            pltpu.VMEM(wind.shape, F32),
            pltpu.SMEM(owner.shape, jnp.int32),
            pltpu.SMEM((SUBS,), jnp.int32),
            pltpu.SMEM(fuel_rate.shape, F32),
            pltpu.SMEM(fuel_wind.shape, F32),
            pltpu.SMEM(fuel_heat.shape, F32),
            pltpu.SemaphoreType.DMA((cols + 1,)),
            pltpu.SemaphoreType.DMA((6,)),
            pltpu.SemaphoreType.DMA((SUBS, 4)),
            pltpu.SemaphoreType.DMA((SUBS, 4)),
            pltpu.SemaphoreType.DMA((4,)),
            pltpu.SemaphoreType.DMA((cols,)),
        ],
        compiler_params=pltpu.CompilerParams(
            collective_id=0, has_side_effects=True, vmem_limit_bytes=60 * 1024 * 1024
        ),
    )(level_set, fuel, wind, owner, active.reshape(SUBS), fuel_rate, fuel_wind, fuel_heat)


def solution(mesh):
    in_specs = (
        P("grp", "tile"),
        P("grp", "tile"),
        P(None, "grp", "tile"),
        P("grp", None),
        P(None, "grp", "tile"),
        P(),
        P(),
        P(),
    )
    out_specs = (P("grp", "tile"), P(None, "grp", "tile"))
    body = functools.partial(shards, mesh.shape["grp"], mesh.shape["tile"])
    return jax.shard_map(body, mesh=mesh, in_specs=in_specs, out_specs=out_specs, check_vma=False)
```

```python
import functools

import jax
import jax.numpy as jnp
from jax import lax
from jax.experimental import pallas as pl
from jax.experimental.pallas import tpu as pltpu
from jax.sharding import PartitionSpec as P

STEPS = 2
SUBSTEPS = 2
SUBS = STEPS * SUBSTEPS
MESH = pl.DeviceIdType.MESH
LANES = 128
PARTS = 8
ROWS = 8
F32 = jnp.float32
BF16 = jnp.bfloat16


def thirds(x):
    high = x.astype(BF16)
    rest = x - high.astype(F32)
    middle = rest.astype(BF16)
    low = (rest - middle.astype(F32)).astype(BF16)
    return [high, middle, low]


def exact_dots(arrays, right):
    pieces = [piece for x in arrays for piece in thirds(x)]
    full = jnp.dot(jnp.concatenate(pieces, axis=0), right, preferred_element_type=F32)
    m = arrays[0].shape[0]
    return [
        full[3 * i * m : (3 * i + 1) * m] + full[(3 * i + 1) * m : (3 * i + 2) * m] + full[(3 * i + 2) * m : (3 * i + 3) * m]
        for i in range(len(arrays))
    ]


def kernel(
    grps, tiles, atm_rows, atm_cols,
    level_ref, fuel_ref, wind_any, owner_any, active_any, rate_any, drift_any, heat_any,
    level_out, wind_out,
    lev_a, lev_b, fuel, rate, drift, heat, burn, row_sums, gust, spread, gather_cols,
    send, halo, wind_first, wind_last, slots_first, slots_last,
    wind_ref, owner_ref, active_ref, rate_tab, wind_tab, heat_tab,
    load_sem, small_sem, send_sem, recv_sem, wind_sem, out_sem,
):
    cell_rows, cell_cols = fuel.shape
    refine = cell_rows // atm_rows
    cols = cell_cols // LANES
    group = 2 * refine
    tiles_in = group // ROWS
    groups = cell_rows // group
    g, t = lax.axis_index("grp"), lax.axis_index("tile")

    barrier = pltpu.get_barrier_semaphore()
    for d in range(1, tiles):
        pl.semaphore_signal(barrier, inc=1, device_id=(g, lax.rem(t + d, tiles)), device_id_type=MESH)

    @pl.when(g > 0)
    def _():
        pl.semaphore_signal(barrier, inc=1, device_id=(g - 1, t), device_id_type=MESH)

    @pl.when(g < grps - 1)
    def _():
        pl.semaphore_signal(barrier, inc=1, device_id=(g + 1, t), device_id_type=MESH)

    load_level = [
        pltpu.make_async_copy(
            level_ref.at[:, pl.ds(c * LANES, LANES)], lev_a.at[c, pl.ds(ROWS, cell_rows), :], load_sem.at[c]
        )
        for c in range(cols)
    ]
    load_fuel = pltpu.make_async_copy(fuel_ref, fuel, load_sem.at[cols])
    outer, inner = (0, cols - 1), tuple(range(1, cols - 1))
    small = [
        pltpu.make_async_copy(source, target, small_sem.at[i])
        for i, (source, target) in enumerate((
            (wind_any, wind_ref), (owner_any, owner_ref), (active_any, active_ref),
            (rate_any, rate_tab), (drift_any, wind_tab), (heat_any, heat_tab),
        ))
    ]
    for copy in small:
        copy.start()
    for c in outer + inner:
        load_level[c].start()
    load_fuel.start()

    lane = lax.broadcasted_iota(jnp.int32, (ROWS, LANES), 1)
    sub = lax.broadcasted_iota(jnp.int32, (ROWS, LANES), 0)
    lane16 = lax.broadcasted_iota(jnp.int32, (atm_rows, LANES), 1)
    sub16 = lax.broadcasted_iota(jnp.int32, (atm_rows, LANES), 0)
    quarter = atm_cols

    def pack(east, north):
        top, low = slice(0, ROWS), slice(ROWS, 2 * ROWS)
        return jnp.where(
            lane < quarter, east[top],
            jnp.where(
                lane < 2 * quarter, pltpu.roll(east[low], quarter, 1),
                jnp.where(lane < 3 * quarter, pltpu.roll(north[top], 2 * quarter, 1), pltpu.roll(north[low], 3 * quarter, 1)),
            ),
        )

    def unpack(packed):
        east = jnp.concatenate([packed, pltpu.roll(packed, 3 * quarter, 1)], axis=0)
        north = jnp.concatenate([pltpu.roll(packed, 2 * quarter, 1), pltpu.roll(packed, quarter, 1)], axis=0)
        return east, north

    def share(packed, source, slots, index):
        source[...] = packed
        slots[t] = packed
        for d in range(1, tiles):
            pltpu.make_async_remote_copy(
                src_ref=source, dst_ref=slots.at[t],
                send_sem=wind_sem.at[2 * index], recv_sem=wind_sem.at[2 * index + 1],
                device_id=(g, lax.rem(t + d, tiles)), device_id_type=MESH,
            ).start()

    def await_all(slots, sem):
        others = slots.at[pl.ds(0, tiles - 1)]
        pltpu.make_async_copy(others, others, sem).wait()

    def halo_copy(k, side, there):
        return pltpu.make_async_remote_copy(
            src_ref=send.at[k, side], dst_ref=halo.at[k, side],
            send_sem=send_sem.at[k, side], recv_sem=recv_sem.at[k, side],
            device_id=there, device_id_type=MESH,
        )

    going = (t < tiles - 1, t > 0, g < grps - 1, g > 0)
    coming = (t > 0, t < tiles - 1, g > 0, g < grps - 1)
    targets = ((g, t + 1), (g, t - 1), (g + 1, t), (g - 1, t))

    def start_sides(k, sides):
        for side in sides:
            @pl.when(going[side])
            def _(side=side):
                halo_copy(k, side, targets[side]).start()

            @pl.when(jnp.logical_not(coming[side]))
            def _(side=side):
                halo[k, side] = send[k, side ^ 1]

    def wait_sides(k):
        for side in range(4):
            @pl.when(coming[side])
            def _(side=side):
                halo_copy(k, side, targets[side ^ 1]).wait_recv()

    def start_columns(k, west_col, east_col):
        send[k, 1] = west_col
        send[k, 0] = east_col
        start_sides(k, (0, 1))

    def start_rows(k, level):
        for side, row in ((2, ROWS + cell_rows - 1), (3, ROWS)):
            send[k, side] = jnp.zeros((ROWS, LANES), F32)
            for c in range(cols):
                send[k, side, c : c + 1, :] = level[c, row : row + 1, :]
        start_sides(k, (2, 3))

    def place_rows(k, level):
        for side, row in ((2, ROWS - 1), (3, ROWS + cell_rows)):
            for c in range(cols):
                level[c, row : row + 1, :] = halo[k, side, c : c + 1, :]

    def columns_into(packs, k, first, last):
        west_pack, east_pack = packs
        west_pack = jnp.where(lane == k, pltpu.roll(first, k, 1), west_pack)
        east_pack = jnp.where(lane == k, pltpu.roll(last, k + 1, 1), east_pack)
        return west_pack, east_pack

    index = lax.broadcasted_iota(jnp.int32, spread.shape, 0) * refine
    place = lax.broadcasted_iota(jnp.int32, spread.shape, 1)
    spread[...] = jnp.where((place >= index) & (place < index + refine), 1.0, 0.0).astype(BF16)
    index = lax.broadcasted_iota(jnp.int32, gather_cols.shape, 1) * refine
    place = lax.broadcasted_iota(jnp.int32, gather_cols.shape, 0)
    gather_cols[...] = jnp.where((place >= index) & (place < index + refine), 1.0, 0.0).astype(BF16)

    def table(ref):
        values = jnp.zeros((ROWS, LANES), F32)
        for category in range(ref.shape[0]):
            values = jnp.where(lane == category, ref[category], values)
        return values

    for copy in small:
        copy.wait()
    tables = [table(ref) for ref in (rate_tab, wind_tab, heat_tab)]
    blank = jnp.zeros((atm_rows, LANES - atm_cols), F32)
    mine = [jnp.concatenate([wind_ref[i], blank], axis=1) for i in range(2)]
    packed_wind = pack(mine[0], mine[1])

    pl.semaphore_wait(barrier, tiles - 1 + (g > 0).astype(jnp.int32) + (g < grps - 1).astype(jnp.int32))
    share(packed_wind, wind_first, slots_first, 0)
    empty = jnp.zeros((ROWS, LANES), F32)
    packs = (empty, empty)
    for c in outer:
        load_level[c].wait()
    for k in range(cell_rows // ROWS):
        rows = pl.ds(ROWS + k * ROWS, ROWS)
        packs = columns_into(packs, k, lev_a[0, rows, :], lev_a[cols - 1, rows, :])
    start_columns(0, *packs)
    for c in inner:
        load_level[c].wait()
    start_rows(0, lev_a)

    load_fuel.wait()

    def prepare(i, carry):
        for q in range(tiles_in):
            start = pl.multiple_of((i * tiles_in + q) * ROWS, ROWS)
            rows = pl.ds(start, ROWS)
            for c in range(cols):
                at = slice(c * LANES, (c + 1) * LANES)
                category = fuel[rows, at]
                for values, out in zip(tables, (rate, drift, heat)):
                    out[rows, at] = jnp.take_along_axis(values, category, axis=1, mode="promise_in_bounds")
                burn[rows, at] = jnp.tanh(lev_a[c, pl.ds(pl.multiple_of(start + ROWS, ROWS), ROWS), :])
        return carry

    lax.fori_loop(0, groups, prepare, 0, unroll=2)

    def expand(east, north):
        wide = exact_dots([east, north], spread[...])
        for part in range(2):
            for c in range(cols):
                gust[part, c] = wide[part][:, c * LANES : (c + 1) * LANES]

    await_all(slots_first, wind_sem.at[1])
    east, north = unpack(slots_first[owner_ref[0, t]])
    expand(east, north)

    def block(i, k, src, dst, want, packs):
        flux = k % SUBSTEPS == SUBSTEPS - 1
        burning = jnp.where(active_ref[k] > 0, F32(1.0), F32(0.0))
        ends = 0 in want
        if ends:
            west_halo, east_halo = halo[k, 0], halo[k, 1]
        around = sorted({n for c in want for n in (c - 1, c, c + 1) if 0 <= n < cols})
        winds = {}
        for c in want:
            winds[c] = [
                [jnp.broadcast_to(gust[part, c, pl.ds(2 * i + a, 1), :], (ROWS, LANES)) for a in range(2)] for part in range(2)
            ]
        sums = {c: [None, None] for c in want}

        def add(c, a, x):
            sums[c][a] = x if sums[c][a] is None else sums[c][a] + x

        for q in range(tiles_in):
            kk = i * tiles_in + q
            start = pl.multiple_of(kk * ROWS, ROWS)
            rows, padded = pl.ds(start, ROWS), pl.ds(pl.multiple_of(start + ROWS, ROWS), ROWS)
            here = {c: src[c, padded, :] for c in around}
            right = {c: pltpu.roll(here[c], 1, 1) for c in around if c in want or c + 1 in want}
            left = {c: pltpu.roll(here[c], LANES - 1, 1) for c in around if c in want or c - 1 in want}
            if ends:
                right[-1] = pltpu.roll(west_halo, lax.rem(LANES - kk, LANES), 1)
                left[cols] = pltpu.roll(east_halo, LANES - 1 - kk, 1)
            low, high = (q * ROWS) // refine, (q * ROWS + ROWS - 1) // refine
            split = refine * high - q * ROWS
            new_edge = {}
            for c in want:
                at = slice(c * LANES, (c + 1) * LANES)
                level = here[c]
                above = src[c, pl.ds(start + ROWS - 1, ROWS), :]
                below = src[c, pl.ds(start + ROWS + 1, ROWS), :]
                back_x = level - jnp.where(lane == 0, right[c - 1], right[c])
                ahead_x = jnp.where(lane == LANES - 1, left[c + 1], left[c]) - level
                back_y = level - above
                ahead_y = below - level
                square = (
                    jnp.maximum(back_x, 0.0) ** 2 + jnp.minimum(ahead_x, 0.0) ** 2
                    + jnp.maximum(back_y, 0.0) ** 2 + jnp.minimum(ahead_y, 0.0) ** 2 + 1e-12
                )
                slope = square * lax.rsqrt(square)
                if low == high:
                    east_w, north_w = winds[c][0][low], winds[c][1][low]
                else:
                    east_w = jnp.where(sub < split, winds[c][0][low], winds[c][0][high])
                    north_w = jnp.where(sub < split, winds[c][1][low], winds[c][1][high])
                carry = east_w * jnp.where(east_w > 0.0, back_x, ahead_x) + north_w * jnp.where(north_w > 0.0, back_y, ahead_y)
                newer = level - burning * (rate[rows, at] * slope + drift[rows, at] * carry)
                dst[c, padded, :] = newer
                new_edge[c] = newer
                if flux:
                    now = jnp.tanh(newer)
                    released = heat[rows, at] * (burn[rows, at] - now)
                    if k < SUBS - 1:
                        burn[rows, at] = now
                    if low == high:
                        add(c, low, released)
                    else:
                        add(c, low, jnp.where(sub < split, released, 0.0))
                        add(c, high, jnp.where(sub < split, 0.0, released))
            if ends and k < SUBS - 1:
                packs = columns_into(packs, kk, new_edge[0], new_edge[cols - 1])
        if flux:
            for c in want:
                for a in range(2):
                    row_sums[c, pl.ds(pl.multiple_of((2 * i + a) * ROWS, ROWS), ROWS), :] = sums[c][a]
        return packs

    def total_rows(c):
        parts = [row_sums[c, pl.ds(s, atm_rows, stride=ROWS), :] for s in range(ROWS)]
        while len(parts) > 1:
            parts = [one + two for one, two in zip(parts[::2], parts[1::2])]
        return parts[0]

    buffers = (lev_a, lev_b)
    store_level = [
        pltpu.make_async_copy(
            buffers[SUBS % 2].at[c, pl.ds(ROWS, cell_rows), :], level_out.at[:, pl.ds(c * LANES, LANES)], out_sem.at[c]
        )
        for c in range(cols)
    ]
    for k in range(SUBS):
        src, dst = buffers[k % 2], buffers[(k + 1) % 2]
        wait_sides(k)
        place_rows(k, src)
        packs = lax.fori_loop(0, groups, lambda i, p: block(i, k, src, dst, outer, p), (empty, empty), unroll=2)
        if k < SUBS - 1:
            start_columns(k + 1, *packs)
        else:
            for c in outer:
                store_level[c].start()

        def middle(i, carry):
            block(i, k, src, dst, inner, None)
            return carry

        lax.fori_loop(0, 2, lambda n, carry: middle(n * (groups - 1), carry), 0, unroll=2)
        if k < SUBS - 1:
            start_rows(k + 1, dst)
        lax.fori_loop(1, groups - 1, middle, 0, unroll=2)
        if k == SUBS - 1:
            for c in inner:
                store_level[c].start()
        if k % SUBSTEPS == SUBSTEPS - 1:
            coarse = exact_dots([jnp.concatenate([total_rows(c) for c in range(cols)], axis=1)], gather_cols[...])[0] * F32(0.5 / (refine * refine))
            west = jnp.where(lane16 == 0, coarse, pltpu.roll(coarse, 1, 1))
            east_c = jnp.where(lane16 == atm_cols - 1, coarse, pltpu.roll(coarse, LANES - 1, 1))
            up = jnp.where(sub16 == 0, coarse, pltpu.roll(coarse, 1, 0))
            down = jnp.where(sub16 == atm_rows - 1, coarse, pltpu.roll(coarse, atm_rows - 1, 0))
            east = 0.9 * east + 40.0 * ((east_c - west) * 0.5)
            north = 0.9 * north + 40.0 * ((down - up) * 0.5)
            if k < SUBS - 1:
                expand(east, north)

    share(pack(east, north), wind_last, slots_last, 1)
    source = jnp.int32(0)
    for j in range(tiles):
        source = jnp.where(owner_ref[0, j] == t, jnp.int32(j), source)
    await_all(slots_last, wind_sem.at[3])
    east, north = unpack(slots_last[source])
    wind_out[0] = east[:, :atm_cols]
    wind_out[1] = north[:, :atm_cols]
    for copy in store_level:
        copy.wait()
    await_all(slots_first, wind_sem.at[0])
    await_all(slots_last, wind_sem.at[2])
    for k in range(SUBS):
        for side in range(4):
            @pl.when(going[side])
            def _(k=k, side=side):
                halo_copy(k, side, targets[side]).wait_send()


def hand_out(level, held, level_out, wind_out, sem):
    rows = level.shape[0] // PARTS
    copies = [pltpu.make_async_copy(held, wind_out, sem.at[PARTS])]
    for i in range(PARTS):
        part = pl.ds(i * rows, rows)
        copies.append(pltpu.make_async_copy(level.at[part, :], level_out.at[part, :], sem.at[i]))
    for copy in copies:
        copy.start()
    for copy in copies:
        copy.wait()


def shards(grps, tiles, level_set, fuel, wind, owner, active, fuel_rate, fuel_wind, fuel_heat):
    cell_rows, cell_cols = level_set.shape
    atm_rows, atm_cols = wind.shape[1], wind.shape[2]
    cells = pltpu.VMEM((cell_rows, cell_cols), F32)
    cols = cell_cols // LANES
    padded = pltpu.VMEM((cols, cell_rows + 2 * ROWS, LANES), F32)
    tile = (ROWS, LANES)
    vmem = pl.BlockSpec(memory_space=pltpu.VMEM)
    anywhere = pl.BlockSpec(memory_space=pl.ANY)
    level, held = pl.pallas_call(
        functools.partial(kernel, grps, tiles, atm_rows, atm_cols),
        out_shape=(jax.ShapeDtypeStruct(level_set.shape, F32), jax.ShapeDtypeStruct(wind.shape, F32)),
        in_specs=[anywhere] * 8,
        out_specs=(anywhere, vmem),
        scratch_shapes=[
            padded, padded,
            pltpu.VMEM((cell_rows, cell_cols), jnp.int32),
            cells, cells, cells, cells,
            pltpu.VMEM((cols, atm_rows * ROWS, LANES), F32),
            pltpu.VMEM((2, cols, atm_rows, LANES), F32),
            pltpu.VMEM((LANES, cell_cols), BF16),
            pltpu.VMEM((cell_cols, LANES), BF16),
            pltpu.VMEM((SUBS, 4) + tile, F32),
            pltpu.VMEM((SUBS, 4) + tile, F32),
            pltpu.VMEM(tile, F32),
            pltpu.VMEM(tile, F32),
            pltpu.VMEM((tiles,) + tile, F32),
            pltpu.VMEM((tiles,) + tile, F32),
            pltpu.VMEM(wind.shape, F32),
            pltpu.SMEM(owner.shape, jnp.int32),
            pltpu.SMEM((SUBS,), jnp.int32),
            pltpu.SMEM(fuel_rate.shape, F32),
            pltpu.SMEM(fuel_wind.shape, F32),
            pltpu.SMEM(fuel_heat.shape, F32),
            pltpu.SemaphoreType.DMA((cols + 1,)),
            pltpu.SemaphoreType.DMA((6,)),
            pltpu.SemaphoreType.DMA((SUBS, 4)),
            pltpu.SemaphoreType.DMA((SUBS, 4)),
            pltpu.SemaphoreType.DMA((4,)),
            pltpu.SemaphoreType.DMA((cols,)),
        ],
        compiler_params=pltpu.CompilerParams(
            collective_id=0, has_side_effects=True, vmem_limit_bytes=60 * 1024 * 1024
        ),
    )(level_set, fuel, wind, owner, active.reshape(SUBS), fuel_rate, fuel_wind, fuel_heat)

    return pl.pallas_call(
        hand_out,
        out_shape=(jax.ShapeDtypeStruct(level_set.shape, F32), jax.ShapeDtypeStruct(wind.shape, F32)),
        in_specs=[anywhere] * 2,
        out_specs=(anywhere, anywhere),
        scratch_shapes=[pltpu.SemaphoreType.DMA((PARTS + 1,))],
        compiler_params=pltpu.CompilerParams(vmem_limit_bytes=60 * 1024 * 1024),
    )(level, held)


def solution(mesh):
    in_specs = (
        P("grp", "tile"),
        P("grp", "tile"),
        P(None, "grp", "tile"),
        P("grp", None),
        P(None, "grp", "tile"),
        P(),
        P(),
        P(),
    )
    out_specs = (P("grp", "tile"), P(None, "grp", "tile"))
    body = functools.partial(shards, mesh.shape["grp"], mesh.shape["tile"])
    return jax.shard_map(body, mesh=mesh, in_specs=in_specs, out_specs=out_specs, check_vma=False)
```

```python
import functools

import jax
import jax.numpy as jnp
from jax import lax
from jax.experimental import pallas as pl
from jax.experimental.pallas import tpu as pltpu
from jax.sharding import PartitionSpec as P

STEPS = 2
SUBSTEPS = 2
SUBS = STEPS * SUBSTEPS
MESH = pl.DeviceIdType.MESH
LANES = 128
PARTS = 4
ROWS = 8
F32 = jnp.float32
BF16 = jnp.bfloat16


def thirds(x):
    high = x.astype(BF16)
    rest = x - high.astype(F32)
    middle = rest.astype(BF16)
    low = (rest - middle.astype(F32)).astype(BF16)
    return [high, middle, low]


def exact_dots(arrays, right):
    pieces = [piece for x in arrays for piece in thirds(x)]
    full = jnp.dot(jnp.concatenate(pieces, axis=0), right, preferred_element_type=F32)
    m = arrays[0].shape[0]
    return [
        full[3 * i * m : (3 * i + 1) * m] + full[(3 * i + 1) * m : (3 * i + 2) * m] + full[(3 * i + 2) * m : (3 * i + 3) * m]
        for i in range(len(arrays))
    ]


def kernel(
    grps, tiles, atm_rows, atm_cols,
    level_ref, fuel_ref, wind_any, owner_any, active_any, rate_any, drift_any, heat_any,
    level_out, wind_out,
    lev_a, lev_b, fuel, rate, drift, heat, burn, row_sums, gust, spread, gather_cols,
    send, halo, wind_first, wind_last, slots_first, slots_last,
    wind_ref, owner_ref, active_ref, rate_tab, wind_tab, heat_tab,
    load_sem, small_sem, send_sem, recv_sem, wind_sem, out_sem,
):
    cell_rows, cell_cols = fuel.shape
    refine = cell_rows // atm_rows
    cols = cell_cols // LANES
    group = 2 * refine
    tiles_in = group // ROWS
    groups = cell_rows // group
    g, t = lax.axis_index("grp"), lax.axis_index("tile")

    barrier = pltpu.get_barrier_semaphore()
    for d in range(1, tiles):
        pl.semaphore_signal(barrier, inc=1, device_id=(g, lax.rem(t + d, tiles)), device_id_type=MESH)

    @pl.when(g > 0)
    def _():
        pl.semaphore_signal(barrier, inc=1, device_id=(g - 1, t), device_id_type=MESH)

    @pl.when(g < grps - 1)
    def _():
        pl.semaphore_signal(barrier, inc=1, device_id=(g + 1, t), device_id_type=MESH)

    load_level = [
        pltpu.make_async_copy(
            level_ref.at[:, pl.ds(c * LANES, LANES)], lev_a.at[c, pl.ds(ROWS, cell_rows), :], load_sem.at[c]
        )
        for c in range(cols)
    ]
    load_fuel = pltpu.make_async_copy(fuel_ref, fuel, load_sem.at[cols])
    outer, inner = (0, cols - 1), tuple(range(1, cols - 1))
    small = [
        pltpu.make_async_copy(source, target, small_sem.at[i])
        for i, (source, target) in enumerate((
            (wind_any, wind_ref), (owner_any, owner_ref), (active_any, active_ref),
            (rate_any, rate_tab), (drift_any, wind_tab), (heat_any, heat_tab),
        ))
    ]
    for copy in small:
        copy.start()
    for c in outer + inner:
        load_level[c].start()
    load_fuel.start()

    lane = lax.broadcasted_iota(jnp.int32, (ROWS, LANES), 1)
    sub = lax.broadcasted_iota(jnp.int32, (ROWS, LANES), 0)
    lane16 = lax.broadcasted_iota(jnp.int32, (atm_rows, LANES), 1)
    sub16 = lax.broadcasted_iota(jnp.int32, (atm_rows, LANES), 0)
    quarter = atm_cols

    def pack(east, north):
        top, low = slice(0, ROWS), slice(ROWS, 2 * ROWS)
        return jnp.where(
            lane < quarter, east[top],
            jnp.where(
                lane < 2 * quarter, pltpu.roll(east[low], quarter, 1),
                jnp.where(lane < 3 * quarter, pltpu.roll(north[top], 2 * quarter, 1), pltpu.roll(north[low], 3 * quarter, 1)),
            ),
        )

    def unpack(packed):
        east = jnp.concatenate([packed, pltpu.roll(packed, 3 * quarter, 1)], axis=0)
        north = jnp.concatenate([pltpu.roll(packed, 2 * quarter, 1), pltpu.roll(packed, quarter, 1)], axis=0)
        return east, north

    def share(packed, source, slots, index):
        source[...] = packed
        slots[t] = packed
        for d in range(1, tiles):
            pltpu.make_async_remote_copy(
                src_ref=source, dst_ref=slots.at[t],
                send_sem=wind_sem.at[2 * index], recv_sem=wind_sem.at[2 * index + 1],
                device_id=(g, lax.rem(t + d, tiles)), device_id_type=MESH,
            ).start()

    def await_all(slots, sem):
        others = slots.at[pl.ds(0, tiles - 1)]
        pltpu.make_async_copy(others, others, sem).wait()

    def halo_copy(k, side, there):
        return pltpu.make_async_remote_copy(
            src_ref=send.at[k, side], dst_ref=halo.at[k, side],
            send_sem=send_sem.at[k, side], recv_sem=recv_sem.at[k, side],
            device_id=there, device_id_type=MESH,
        )

    going = (t < tiles - 1, t > 0, g < grps - 1, g > 0)
    coming = (t > 0, t < tiles - 1, g > 0, g < grps - 1)
    targets = ((g, t + 1), (g, t - 1), (g + 1, t), (g - 1, t))

    def start_sides(k, sides):
        for side in sides:
            @pl.when(going[side])
            def _(side=side):
                halo_copy(k, side, targets[side]).start()

            @pl.when(jnp.logical_not(coming[side]))
            def _(side=side):
                halo[k, side] = send[k, side ^ 1]

    def wait_sides(k):
        for side in range(4):
            @pl.when(coming[side])
            def _(side=side):
                halo_copy(k, side, targets[side ^ 1]).wait_recv()

    def start_columns(k, west_col, east_col):
        send[k, 1] = west_col
        send[k, 0] = east_col
        start_sides(k, (0, 1))

    def start_rows(k, level):
        for side, row in ((2, ROWS + cell_rows - 1), (3, ROWS)):
            send[k, side] = jnp.zeros((ROWS, LANES), F32)
            for c in range(cols):
                send[k, side, c : c + 1, :] = level[c, row : row + 1, :]
        start_sides(k, (2, 3))

    def place_rows(k, level):
        for side, row in ((2, ROWS - 1), (3, ROWS + cell_rows)):
            for c in range(cols):
                level[c, row : row + 1, :] = halo[k, side, c : c + 1, :]

    def columns_into(packs, k, first, last):
        west_pack, east_pack = packs
        west_pack = jnp.where(lane == k, pltpu.roll(first, k, 1), west_pack)
        east_pack = jnp.where(lane == k, pltpu.roll(last, k + 1, 1), east_pack)
        return west_pack, east_pack

    index = lax.broadcasted_iota(jnp.int32, spread.shape, 0) * refine
    place = lax.broadcasted_iota(jnp.int32, spread.shape, 1)
    spread[...] = jnp.where((place >= index) & (place < index + refine), 1.0, 0.0).astype(BF16)
    index = lax.broadcasted_iota(jnp.int32, gather_cols.shape, 1) * refine
    place = lax.broadcasted_iota(jnp.int32, gather_cols.shape, 0)
    gather_cols[...] = jnp.where((place >= index) & (place < index + refine), 1.0, 0.0).astype(BF16)

    def table(ref):
        values = jnp.zeros((ROWS, LANES), F32)
        for category in range(ref.shape[0]):
            values = jnp.where(lane == category, ref[category], values)
        return values

    for copy in small:
        copy.wait()
    tables = [table(ref) for ref in (rate_tab, wind_tab, heat_tab)]
    blank = jnp.zeros((atm_rows, LANES - atm_cols), F32)
    mine = [jnp.concatenate([wind_ref[i], blank], axis=1) for i in range(2)]
    packed_wind = pack(mine[0], mine[1])

    pl.semaphore_wait(barrier, tiles - 1 + (g > 0).astype(jnp.int32) + (g < grps - 1).astype(jnp.int32))
    share(packed_wind, wind_first, slots_first, 0)
    empty = jnp.zeros((ROWS, LANES), F32)
    packs = (empty, empty)
    for c in outer:
        load_level[c].wait()
    for k in range(cell_rows // ROWS):
        rows = pl.ds(ROWS + k * ROWS, ROWS)
        packs = columns_into(packs, k, lev_a[0, rows, :], lev_a[cols - 1, rows, :])
    start_columns(0, *packs)
    for c in inner:
        load_level[c].wait()
    start_rows(0, lev_a)

    load_fuel.wait()

    def prepare(i, carry):
        for q in range(tiles_in):
            start = pl.multiple_of((i * tiles_in + q) * ROWS, ROWS)
            rows = pl.ds(start, ROWS)
            for c in range(cols):
                at = slice(c * LANES, (c + 1) * LANES)
                category = fuel[rows, at]
                for values, out in zip(tables, (rate, drift, heat)):
                    out[rows, at] = jnp.take_along_axis(values, category, axis=1, mode="promise_in_bounds")
                burn[rows, at] = jnp.tanh(lev_a[c, pl.ds(pl.multiple_of(start + ROWS, ROWS), ROWS), :])
        return carry

    lax.fori_loop(0, groups, prepare, 0, unroll=2)

    def expand(east, north):
        wide = exact_dots([east, north], spread[...])
        for part in range(2):
            for c in range(cols):
                gust[part, c] = wide[part][:, c * LANES : (c + 1) * LANES]

    await_all(slots_first, wind_sem.at[1])
    east, north = unpack(slots_first[owner_ref[0, t]])
    expand(east, north)

    def block(i, k, src, dst, want, packs):
        flux = k % SUBSTEPS == SUBSTEPS - 1
        burning = jnp.where(active_ref[k] > 0, F32(1.0), F32(0.0))
        ends = 0 in want
        if ends:
            west_halo, east_halo = halo[k, 0], halo[k, 1]
        around = sorted({n for c in want for n in (c - 1, c, c + 1) if 0 <= n < cols})
        winds = {}
        for c in want:
            winds[c] = [
                [jnp.broadcast_to(gust[part, c, pl.ds(2 * i + a, 1), :], (ROWS, LANES)) for a in range(2)] for part in range(2)
            ]
        sums = {c: [None, None] for c in want}

        def add(c, a, x):
            sums[c][a] = x if sums[c][a] is None else sums[c][a] + x

        for q in range(tiles_in):
            kk = i * tiles_in + q
            start = pl.multiple_of(kk * ROWS, ROWS)
            rows, padded = pl.ds(start, ROWS), pl.ds(pl.multiple_of(start + ROWS, ROWS), ROWS)
            here = {c: src[c, padded, :] for c in around}
            right = {c: pltpu.roll(here[c], 1, 1) for c in around if c in want or c + 1 in want}
            left = {c: pltpu.roll(here[c], LANES - 1, 1) for c in around if c in want or c - 1 in want}
            if ends:
                right[-1] = pltpu.roll(west_halo, lax.rem(LANES - kk, LANES), 1)
                left[cols] = pltpu.roll(east_halo, LANES - 1 - kk, 1)
            low, high = (q * ROWS) // refine, (q * ROWS + ROWS - 1) // refine
            split = refine * high - q * ROWS
            new_edge = {}
            for c in want:
                at = slice(c * LANES, (c + 1) * LANES)
                level = here[c]
                above = src[c, pl.ds(start + ROWS - 1, ROWS), :]
                below = src[c, pl.ds(start + ROWS + 1, ROWS), :]
                back_x = level - jnp.where(lane == 0, right[c - 1], right[c])
                ahead_x = jnp.where(lane == LANES - 1, left[c + 1], left[c]) - level
                back_y = level - above
                ahead_y = below - level
                square = (
                    jnp.maximum(back_x, 0.0) ** 2 + jnp.minimum(ahead_x, 0.0) ** 2
                    + jnp.maximum(back_y, 0.0) ** 2 + jnp.minimum(ahead_y, 0.0) ** 2 + 1e-12
                )
                slope = square * lax.rsqrt(square)
                if low == high:
                    east_w, north_w = winds[c][0][low], winds[c][1][low]
                else:
                    east_w = jnp.where(sub < split, winds[c][0][low], winds[c][0][high])
                    north_w = jnp.where(sub < split, winds[c][1][low], winds[c][1][high])
                carry = east_w * jnp.where(east_w > 0.0, back_x, ahead_x) + north_w * jnp.where(north_w > 0.0, back_y, ahead_y)
                newer = level - burning * (rate[rows, at] * slope + drift[rows, at] * carry)
                dst[c, padded, :] = newer
                new_edge[c] = newer
                if flux:
                    now = jnp.tanh(newer)
                    released = heat[rows, at] * (burn[rows, at] - now)
                    if k < SUBS - 1:
                        burn[rows, at] = now
                    if low == high:
                        add(c, low, released)
                    else:
                        add(c, low, jnp.where(sub < split, released, 0.0))
                        add(c, high, jnp.where(sub < split, 0.0, released))
            if ends and k < SUBS - 1:
                packs = columns_into(packs, kk, new_edge[0], new_edge[cols - 1])
        if flux:
            for c in want:
                for a in range(2):
                    row_sums[c, pl.ds(pl.multiple_of((2 * i + a) * ROWS, ROWS), ROWS), :] = sums[c][a]
        return packs

    def total_rows(c):
        parts = [row_sums[c, pl.ds(s, atm_rows, stride=ROWS), :] for s in range(ROWS)]
        while len(parts) > 1:
            parts = [one + two for one, two in zip(parts[::2], parts[1::2])]
        return parts[0]

    buffers = (lev_a, lev_b)
    store_level = [
        pltpu.make_async_copy(
            buffers[SUBS % 2].at[c, pl.ds(ROWS, cell_rows), :], level_out.at[:, pl.ds(c * LANES, LANES)], out_sem.at[c]
        )
        for c in range(cols)
    ]
    for k in range(SUBS):
        src, dst = buffers[k % 2], buffers[(k + 1) % 2]
        wait_sides(k)
        place_rows(k, src)
        packs = lax.fori_loop(0, groups, lambda i, p: block(i, k, src, dst, outer, p), (empty, empty), unroll=2)
        if k < SUBS - 1:
            start_columns(k + 1, *packs)
        else:
            for c in outer:
                store_level[c].start()

        def middle(i, carry):
            block(i, k, src, dst, inner, None)
            return carry

        lax.fori_loop(0, 2, lambda n, carry: middle(n * (groups - 1), carry), 0, unroll=2)
        if k < SUBS - 1:
            start_rows(k + 1, dst)
        lax.fori_loop(1, groups - 1, middle, 0, unroll=2)
        if k == SUBS - 1:
            for c in inner:
                store_level[c].start()
        if k % SUBSTEPS == SUBSTEPS - 1:
            coarse = exact_dots([jnp.concatenate([total_rows(c) for c in range(cols)], axis=1)], gather_cols[...])[0] * F32(0.5 / (refine * refine))
            west = jnp.where(lane16 == 0, coarse, pltpu.roll(coarse, 1, 1))
            east_c = jnp.where(lane16 == atm_cols - 1, coarse, pltpu.roll(coarse, LANES - 1, 1))
            up = jnp.where(sub16 == 0, coarse, pltpu.roll(coarse, 1, 0))
            down = jnp.where(sub16 == atm_rows - 1, coarse, pltpu.roll(coarse, atm_rows - 1, 0))
            east = 0.9 * east + 40.0 * ((east_c - west) * 0.5)
            north = 0.9 * north + 40.0 * ((down - up) * 0.5)
            if k < SUBS - 1:
                expand(east, north)

    share(pack(east, north), wind_last, slots_last, 1)
    source = jnp.int32(0)
    for j in range(tiles):
        source = jnp.where(owner_ref[0, j] == t, jnp.int32(j), source)
    await_all(slots_last, wind_sem.at[3])
    east, north = unpack(slots_last[source])
    wind_out[0] = east[:, :atm_cols]
    wind_out[1] = north[:, :atm_cols]
    for copy in store_level:
        copy.wait()
    await_all(slots_first, wind_sem.at[0])
    await_all(slots_last, wind_sem.at[2])
    for k in range(SUBS):
        for side in range(4):
            @pl.when(going[side])
            def _(k=k, side=side):
                halo_copy(k, side, targets[side]).wait_send()


def hand_out(level, held, level_out, wind_out, level_held, wind_held, in_sem, out_sem):
    rows = level.shape[0] // PARTS
    views = [(held, wind_held, wind_out)]
    for i in range(PARTS):
        part = pl.ds(i * rows, rows)
        views.append(tuple(ref.at[part, :] for ref in (level, level_held, level_out)))
    inward = [pltpu.make_async_copy(a, b, in_sem.at[i]) for i, (a, b, _) in enumerate(views)]
    outward = [pltpu.make_async_copy(b, c, out_sem.at[i]) for i, (_, b, c) in enumerate(views)]
    for copy in inward:
        copy.start()
    for first, second in zip(inward, outward):
        first.wait()
        second.start()
    for copy in outward:
        copy.wait()


def shards(grps, tiles, level_set, fuel, wind, owner, active, fuel_rate, fuel_wind, fuel_heat):
    cell_rows, cell_cols = level_set.shape
    atm_rows, atm_cols = wind.shape[1], wind.shape[2]
    cells = pltpu.VMEM((cell_rows, cell_cols), F32)
    cols = cell_cols // LANES
    padded = pltpu.VMEM((cols, cell_rows + 2 * ROWS, LANES), F32)
    tile = (ROWS, LANES)
    vmem = pl.BlockSpec(memory_space=pltpu.VMEM)
    anywhere = pl.BlockSpec(memory_space=pl.ANY)
    level, held = pl.pallas_call(
        functools.partial(kernel, grps, tiles, atm_rows, atm_cols),
        out_shape=(jax.ShapeDtypeStruct(level_set.shape, F32), jax.ShapeDtypeStruct(wind.shape, F32)),
        in_specs=[anywhere] * 8,
        out_specs=(anywhere, vmem),
        scratch_shapes=[
            padded, padded,
            pltpu.VMEM((cell_rows, cell_cols), jnp.int32),
            cells, cells, cells, cells,
            pltpu.VMEM((cols, atm_rows * ROWS, LANES), F32),
            pltpu.VMEM((2, cols, atm_rows, LANES), F32),
            pltpu.VMEM((LANES, cell_cols), BF16),
            pltpu.VMEM((cell_cols, LANES), BF16),
            pltpu.VMEM((SUBS, 4) + tile, F32),
            pltpu.VMEM((SUBS, 4) + tile, F32),
            pltpu.VMEM(tile, F32),
            pltpu.VMEM(tile, F32),
            pltpu.VMEM((tiles,) + tile, F32),
            pltpu.VMEM((tiles,) + tile, F32),
            pltpu.VMEM(wind.shape, F32),
            pltpu.SMEM(owner.shape, jnp.int32),
            pltpu.SMEM((SUBS,), jnp.int32),
            pltpu.SMEM(fuel_rate.shape, F32),
            pltpu.SMEM(fuel_wind.shape, F32),
            pltpu.SMEM(fuel_heat.shape, F32),
            pltpu.SemaphoreType.DMA((cols + 1,)),
            pltpu.SemaphoreType.DMA((6,)),
            pltpu.SemaphoreType.DMA((SUBS, 4)),
            pltpu.SemaphoreType.DMA((SUBS, 4)),
            pltpu.SemaphoreType.DMA((4,)),
            pltpu.SemaphoreType.DMA((cols,)),
        ],
        compiler_params=pltpu.CompilerParams(
            collective_id=0, has_side_effects=True, vmem_limit_bytes=60 * 1024 * 1024
        ),
    )(level_set, fuel, wind, owner, active.reshape(SUBS), fuel_rate, fuel_wind, fuel_heat)

    return pl.pallas_call(
        hand_out,
        out_shape=(jax.ShapeDtypeStruct(level_set.shape, F32), jax.ShapeDtypeStruct(wind.shape, F32)),
        in_specs=[anywhere] * 2,
        out_specs=(anywhere, anywhere),
        scratch_shapes=[
            pltpu.VMEM(level_set.shape, F32), pltpu.VMEM(wind.shape, F32),
            pltpu.SemaphoreType.DMA((PARTS + 1,)), pltpu.SemaphoreType.DMA((PARTS + 1,)),
        ],
        compiler_params=pltpu.CompilerParams(vmem_limit_bytes=60 * 1024 * 1024),
    )(level, held)


def solution(mesh):
    in_specs = (
        P("grp", "tile"),
        P("grp", "tile"),
        P(None, "grp", "tile"),
        P("grp", None),
        P(None, "grp", "tile"),
        P(),
        P(),
        P(),
    )
    out_specs = (P("grp", "tile"), P(None, "grp", "tile"))
    body = functools.partial(shards, mesh.shape["grp"], mesh.shape["tile"])
    return jax.shard_map(body, mesh=mesh, in_specs=in_specs, out_specs=out_specs, check_vma=False)
```

```python
import functools

import jax
import jax.numpy as jnp
from jax import lax
from jax.experimental import pallas as pl
from jax.experimental.pallas import tpu as pltpu
from jax.sharding import PartitionSpec as P

STEPS = 2
SUBSTEPS = 2
SUBS = STEPS * SUBSTEPS
MESH = pl.DeviceIdType.MESH
LANES = 128
PARTS = 4
ROWS = 8
F32 = jnp.float32
BF16 = jnp.bfloat16


def thirds(x):
    high = x.astype(BF16)
    rest = x - high.astype(F32)
    middle = rest.astype(BF16)
    low = (rest - middle.astype(F32)).astype(BF16)
    return [high, middle, low]


def exact_dots(arrays, right):
    pieces = [piece for x in arrays for piece in thirds(x)]
    full = jnp.dot(jnp.concatenate(pieces, axis=0), right, preferred_element_type=F32)
    m = arrays[0].shape[0]
    return [
        full[3 * i * m : (3 * i + 1) * m] + full[(3 * i + 1) * m : (3 * i + 2) * m] + full[(3 * i + 2) * m : (3 * i + 3) * m]
        for i in range(len(arrays))
    ]


def kernel(
    grps, tiles, atm_rows, atm_cols,
    level_ref, fuel_ref, wind_any, owner_any, active_any, rate_any, drift_any, heat_any,
    level_out, wind_out,
    lev_a, lev_b, fuel, rate, drift, heat, burn, row_sums, gust, spread, gather_cols,
    send, halo, wind_first, wind_last, slots_first, slots_last,
    wind_ref, owner_ref, active_ref, rate_tab, wind_tab, heat_tab,
    load_sem, small_sem, send_sem, recv_sem, wind_sem, out_sem,
):
    cell_rows, cell_cols = fuel.shape
    refine = cell_rows // atm_rows
    cols = cell_cols // LANES
    group = 2 * refine
    tiles_in = group // ROWS
    groups = cell_rows // group
    g, t = lax.axis_index("grp"), lax.axis_index("tile")

    barrier = pltpu.get_barrier_semaphore()
    for d in range(1, tiles):
        pl.semaphore_signal(barrier, inc=1, device_id=(g, lax.rem(t + d, tiles)), device_id_type=MESH)

    @pl.when(g > 0)
    def _():
        pl.semaphore_signal(barrier, inc=1, device_id=(g - 1, t), device_id_type=MESH)

    @pl.when(g < grps - 1)
    def _():
        pl.semaphore_signal(barrier, inc=1, device_id=(g + 1, t), device_id_type=MESH)

    load_level = [
        pltpu.make_async_copy(
            level_ref.at[:, pl.ds(c * LANES, LANES)], lev_a.at[c, pl.ds(ROWS, cell_rows), :], load_sem.at[c]
        )
        for c in range(cols)
    ]
    load_fuel = pltpu.make_async_copy(fuel_ref, fuel, load_sem.at[cols])
    outer, inner = (0, cols - 1), tuple(range(1, cols - 1))
    small = [
        pltpu.make_async_copy(source, target, small_sem.at[i])
        for i, (source, target) in enumerate((
            (wind_any, wind_ref), (owner_any, owner_ref), (active_any, active_ref),
            (rate_any, rate_tab), (drift_any, wind_tab), (heat_any, heat_tab),
        ))
    ]
    for copy in small:
        copy.start()
    for c in outer + inner:
        load_level[c].start()
    load_fuel.start()

    lane = lax.broadcasted_iota(jnp.int32, (ROWS, LANES), 1)
    sub = lax.broadcasted_iota(jnp.int32, (ROWS, LANES), 0)
    lane16 = lax.broadcasted_iota(jnp.int32, (atm_rows, LANES), 1)
    sub16 = lax.broadcasted_iota(jnp.int32, (atm_rows, LANES), 0)
    quarter = atm_cols

    def pack(east, north):
        top, low = slice(0, ROWS), slice(ROWS, 2 * ROWS)
        return jnp.where(
            lane < quarter, east[top],
            jnp.where(
                lane < 2 * quarter, pltpu.roll(east[low], quarter, 1),
                jnp.where(lane < 3 * quarter, pltpu.roll(north[top], 2 * quarter, 1), pltpu.roll(north[low], 3 * quarter, 1)),
            ),
        )

    def unpack(packed):
        east = jnp.concatenate([packed, pltpu.roll(packed, 3 * quarter, 1)], axis=0)
        north = jnp.concatenate([pltpu.roll(packed, 2 * quarter, 1), pltpu.roll(packed, quarter, 1)], axis=0)
        return east, north

    def share(packed, source, slots, index):
        source[...] = packed
        slots[t] = packed
        for d in range(1, tiles):
            pltpu.make_async_remote_copy(
                src_ref=source, dst_ref=slots.at[t],
                send_sem=wind_sem.at[2 * index], recv_sem=wind_sem.at[2 * index + 1],
                device_id=(g, lax.rem(t + d, tiles)), device_id_type=MESH,
            ).start()

    def await_all(slots, sem):
        others = slots.at[pl.ds(0, tiles - 1)]
        pltpu.make_async_copy(others, others, sem).wait()

    def halo_copy(k, side, there):
        return pltpu.make_async_remote_copy(
            src_ref=send.at[k, side], dst_ref=halo.at[k, side],
            send_sem=send_sem.at[k, side], recv_sem=recv_sem.at[k, side],
            device_id=there, device_id_type=MESH,
        )

    going = (t < tiles - 1, t > 0, g < grps - 1, g > 0)
    coming = (t > 0, t < tiles - 1, g > 0, g < grps - 1)
    targets = ((g, t + 1), (g, t - 1), (g + 1, t), (g - 1, t))

    def start_sides(k, sides):
        for side in sides:
            @pl.when(going[side])
            def _(side=side):
                halo_copy(k, side, targets[side]).start()

            @pl.when(jnp.logical_not(coming[side]))
            def _(side=side):
                halo[k, side] = send[k, side ^ 1]

    def wait_sides(k):
        for side in range(4):
            @pl.when(coming[side])
            def _(side=side):
                halo_copy(k, side, targets[side ^ 1]).wait_recv()

    def start_columns(k, west_col, east_col):
        send[k, 1] = west_col
        send[k, 0] = east_col
        start_sides(k, (0, 1))

    def start_rows(k, level):
        for side, row in ((2, ROWS + cell_rows - 1), (3, ROWS)):
            send[k, side] = jnp.zeros((ROWS, LANES), F32)
            for c in range(cols):
                send[k, side, c : c + 1, :] = level[c, row : row + 1, :]
        start_sides(k, (2, 3))

    def place_rows(k, level):
        for side, row in ((2, ROWS - 1), (3, ROWS + cell_rows)):
            for c in range(cols):
                level[c, row : row + 1, :] = halo[k, side, c : c + 1, :]

    def columns_into(packs, k, first, last):
        west_pack, east_pack = packs
        west_pack = jnp.where(lane == k, pltpu.roll(first, k, 1), west_pack)
        east_pack = jnp.where(lane == k, pltpu.roll(last, k + 1, 1), east_pack)
        return west_pack, east_pack

    index = lax.broadcasted_iota(jnp.int32, spread.shape, 0) * refine
    place = lax.broadcasted_iota(jnp.int32, spread.shape, 1)
    spread[...] = jnp.where((place >= index) & (place < index + refine), 1.0, 0.0).astype(BF16)
    index = lax.broadcasted_iota(jnp.int32, gather_cols.shape, 1) * refine
    place = lax.broadcasted_iota(jnp.int32, gather_cols.shape, 0)
    gather_cols[...] = jnp.where((place >= index) & (place < index + refine), 1.0, 0.0).astype(BF16)

    def table(ref):
        values = jnp.zeros((ROWS, LANES), F32)
        for category in range(ref.shape[0]):
            values = jnp.where(lane == category, ref[category], values)
        return values

    small[0].wait()
    blank = jnp.zeros((atm_rows, LANES - atm_cols), F32)
    mine = [jnp.concatenate([wind_ref[i], blank], axis=1) for i in range(2)]
    packed_wind = pack(mine[0], mine[1])

    pl.semaphore_wait(barrier, tiles - 1 + (g > 0).astype(jnp.int32) + (g < grps - 1).astype(jnp.int32))
    share(packed_wind, wind_first, slots_first, 0)
    empty = jnp.zeros((ROWS, LANES), F32)
    packs = (empty, empty)
    for c in outer:
        load_level[c].wait()
    for k in range(cell_rows // ROWS):
        rows = pl.ds(ROWS + k * ROWS, ROWS)
        packs = columns_into(packs, k, lev_a[0, rows, :], lev_a[cols - 1, rows, :])
    start_columns(0, *packs)
    for c in inner:
        load_level[c].wait()
    start_rows(0, lev_a)

    for copy in small[1:]:
        copy.wait()
    tables = [table(ref) for ref in (rate_tab, wind_tab, heat_tab)]
    load_fuel.wait()

    def prepare(i, carry):
        for q in range(tiles_in):
            start = pl.multiple_of((i * tiles_in + q) * ROWS, ROWS)
            rows = pl.ds(start, ROWS)
            for c in range(cols):
                at = slice(c * LANES, (c + 1) * LANES)
                category = fuel[rows, at]
                for values, out in zip(tables, (rate, drift, heat)):
                    out[rows, at] = jnp.take_along_axis(values, category, axis=1, mode="promise_in_bounds")
                burn[rows, at] = jnp.tanh(lev_a[c, pl.ds(pl.multiple_of(start + ROWS, ROWS), ROWS), :])
        return carry

    lax.fori_loop(0, groups, prepare, 0, unroll=2)

    def expand(east, north):
        wide = exact_dots([east, north], spread[...])
        for part in range(2):
            for c in range(cols):
                gust[part, c] = wide[part][:, c * LANES : (c + 1) * LANES]

    await_all(slots_first, wind_sem.at[1])
    east, north = unpack(slots_first[owner_ref[0, t]])
    expand(east, north)

    def block(i, k, src, dst, want, packs):
        flux = k % SUBSTEPS == SUBSTEPS - 1
        burning = jnp.where(active_ref[k] > 0, F32(1.0), F32(0.0))
        ends = 0 in want
        if ends:
            west_halo, east_halo = halo[k, 0], halo[k, 1]
        around = sorted({n for c in want for n in (c - 1, c, c + 1) if 0 <= n < cols})
        winds = {}
        for c in want:
            winds[c] = [
                [jnp.broadcast_to(gust[part, c, pl.ds(2 * i + a, 1), :], (ROWS, LANES)) for a in range(2)] for part in range(2)
            ]
        sums = {c: [None, None] for c in want}

        def add(c, a, x):
            sums[c][a] = x if sums[c][a] is None else sums[c][a] + x

        for q in range(tiles_in):
            kk = i * tiles_in + q
            start = pl.multiple_of(kk * ROWS, ROWS)
            rows, padded = pl.ds(start, ROWS), pl.ds(pl.multiple_of(start + ROWS, ROWS), ROWS)
            here = {c: src[c, padded, :] for c in around}
            right = {c: pltpu.roll(here[c], 1, 1) for c in around if c in want or c + 1 in want}
            left = {c: pltpu.roll(here[c], LANES - 1, 1) for c in around if c in want or c - 1 in want}
            if ends:
                right[-1] = pltpu.roll(west_halo, lax.rem(LANES - kk, LANES), 1)
                left[cols] = pltpu.roll(east_halo, LANES - 1 - kk, 1)
            low, high = (q * ROWS) // refine, (q * ROWS + ROWS - 1) // refine
            split = refine * high - q * ROWS
            new_edge = {}
            for c in want:
                at = slice(c * LANES, (c + 1) * LANES)
                level = here[c]
                above = src[c, pl.ds(start + ROWS - 1, ROWS), :]
                below = src[c, pl.ds(start + ROWS + 1, ROWS), :]
                back_x = level - jnp.where(lane == 0, right[c - 1], right[c])
                ahead_x = jnp.where(lane == LANES - 1, left[c + 1], left[c]) - level
                back_y = level - above
                ahead_y = below - level
                square = (
                    jnp.maximum(back_x, 0.0) ** 2 + jnp.minimum(ahead_x, 0.0) ** 2
                    + jnp.maximum(back_y, 0.0) ** 2 + jnp.minimum(ahead_y, 0.0) ** 2 + 1e-12
                )
                slope = square * lax.rsqrt(square)
                if low == high:
                    east_w, north_w = winds[c][0][low], winds[c][1][low]
                else:
                    east_w = jnp.where(sub < split, winds[c][0][low], winds[c][0][high])
                    north_w = jnp.where(sub < split, winds[c][1][low], winds[c][1][high])
                carry = east_w * jnp.where(east_w > 0.0, back_x, ahead_x) + north_w * jnp.where(north_w > 0.0, back_y, ahead_y)
                newer = level - burning * (rate[rows, at] * slope + drift[rows, at] * carry)
                dst[c, padded, :] = newer
                new_edge[c] = newer
                if flux:
                    now = jnp.tanh(newer)
                    released = heat[rows, at] * (burn[rows, at] - now)
                    if k < SUBS - 1:
                        burn[rows, at] = now
                    if low == high:
                        add(c, low, released)
                    else:
                        add(c, low, jnp.where(sub < split, released, 0.0))
                        add(c, high, jnp.where(sub < split, 0.0, released))
            if ends and k < SUBS - 1:
                packs = columns_into(packs, kk, new_edge[0], new_edge[cols - 1])
        if flux:
            for c in want:
                for a in range(2):
                    row_sums[c, pl.ds(pl.multiple_of((2 * i + a) * ROWS, ROWS), ROWS), :] = sums[c][a]
        return packs

    def total_rows(c):
        parts = [row_sums[c, pl.ds(s, atm_rows, stride=ROWS), :] for s in range(ROWS)]
        while len(parts) > 1:
            parts = [one + two for one, two in zip(parts[::2], parts[1::2])]
        return parts[0]

    buffers = (lev_a, lev_b)
    store_level = [
        pltpu.make_async_copy(
            buffers[SUBS % 2].at[c, pl.ds(ROWS, cell_rows), :], level_out.at[:, pl.ds(c * LANES, LANES)], out_sem.at[c]
        )
        for c in range(cols)
    ]
    for k in range(SUBS):
        src, dst = buffers[k % 2], buffers[(k + 1) % 2]
        wait_sides(k)
        place_rows(k, src)
        packs = lax.fori_loop(0, groups, lambda i, p: block(i, k, src, dst, outer, p), (empty, empty), unroll=2)
        if k < SUBS - 1:
            start_columns(k + 1, *packs)
        else:
            for c in outer:
                store_level[c].start()

        def middle(i, carry):
            block(i, k, src, dst, inner, None)
            return carry

        lax.fori_loop(0, 2, lambda n, carry: middle(n * (groups - 1), carry), 0, unroll=2)
        if k < SUBS - 1:
            start_rows(k + 1, dst)
        lax.fori_loop(1, groups - 1, middle, 0, unroll=3)
        if k == SUBS - 1:
            for c in inner:
                store_level[c].start()
        if k % SUBSTEPS == SUBSTEPS - 1:
            coarse = exact_dots([jnp.concatenate([total_rows(c) for c in range(cols)], axis=1)], gather_cols[...])[0] * F32(0.5 / (refine * refine))
            west = jnp.where(lane16 == 0, coarse, pltpu.roll(coarse, 1, 1))
            east_c = jnp.where(lane16 == atm_cols - 1, coarse, pltpu.roll(coarse, LANES - 1, 1))
            up = jnp.where(sub16 == 0, coarse, pltpu.roll(coarse, 1, 0))
            down = jnp.where(sub16 == atm_rows - 1, coarse, pltpu.roll(coarse, atm_rows - 1, 0))
            east = 0.9 * east + 40.0 * ((east_c - west) * 0.5)
            north = 0.9 * north + 40.0 * ((down - up) * 0.5)
            if k < SUBS - 1:
                expand(east, north)

    share(pack(east, north), wind_last, slots_last, 1)
    source = jnp.int32(0)
    for j in range(tiles):
        source = jnp.where(owner_ref[0, j] == t, jnp.int32(j), source)
    await_all(slots_last, wind_sem.at[3])
    east, north = unpack(slots_last[source])
    wind_out[0] = east[:, :atm_cols]
    wind_out[1] = north[:, :atm_cols]
    for copy in store_level:
        copy.wait()
    await_all(slots_first, wind_sem.at[0])
    await_all(slots_last, wind_sem.at[2])
    for k in range(SUBS):
        for side in range(4):
            @pl.when(going[side])
            def _(k=k, side=side):
                halo_copy(k, side, targets[side]).wait_send()


def hand_out(level, held, level_out, wind_out, level_held, wind_held, in_sem, out_sem):
    rows = level.shape[0] // PARTS
    views = [(held, wind_held, wind_out)]
    for i in range(PARTS):
        part = pl.ds(i * rows, rows)
        views.append(tuple(ref.at[part, :] for ref in (level, level_held, level_out)))
    inward = [pltpu.make_async_copy(a, b, in_sem.at[i]) for i, (a, b, _) in enumerate(views)]
    outward = [pltpu.make_async_copy(b, c, out_sem.at[i]) for i, (_, b, c) in enumerate(views)]
    for copy in inward:
        copy.start()
    for first, second in zip(inward, outward):
        first.wait()
        second.start()
    for copy in outward:
        copy.wait()


def shards(grps, tiles, level_set, fuel, wind, owner, active, fuel_rate, fuel_wind, fuel_heat):
    cell_rows, cell_cols = level_set.shape
    atm_rows, atm_cols = wind.shape[1], wind.shape[2]
    cells = pltpu.VMEM((cell_rows, cell_cols), F32)
    cols = cell_cols // LANES
    padded = pltpu.VMEM((cols, cell_rows + 2 * ROWS, LANES), F32)
    tile = (ROWS, LANES)
    vmem = pl.BlockSpec(memory_space=pltpu.VMEM)
    anywhere = pl.BlockSpec(memory_space=pl.ANY)
    level, held = pl.pallas_call(
        functools.partial(kernel, grps, tiles, atm_rows, atm_cols),
        out_shape=(jax.ShapeDtypeStruct(level_set.shape, F32), jax.ShapeDtypeStruct(wind.shape, F32)),
        in_specs=[anywhere] * 8,
        out_specs=(anywhere, vmem),
        scratch_shapes=[
            padded, padded,
            pltpu.VMEM((cell_rows, cell_cols), jnp.int32),
            cells, cells, cells, cells,
            pltpu.VMEM((cols, atm_rows * ROWS, LANES), F32),
            pltpu.VMEM((2, cols, atm_rows, LANES), F32),
            pltpu.VMEM((LANES, cell_cols), BF16),
            pltpu.VMEM((cell_cols, LANES), BF16),
            pltpu.VMEM((SUBS, 4) + tile, F32),
            pltpu.VMEM((SUBS, 4) + tile, F32),
            pltpu.VMEM(tile, F32),
            pltpu.VMEM(tile, F32),
            pltpu.VMEM((tiles,) + tile, F32),
            pltpu.VMEM((tiles,) + tile, F32),
            pltpu.VMEM(wind.shape, F32),
            pltpu.SMEM(owner.shape, jnp.int32),
            pltpu.SMEM((SUBS,), jnp.int32),
            pltpu.SMEM(fuel_rate.shape, F32),
            pltpu.SMEM(fuel_wind.shape, F32),
            pltpu.SMEM(fuel_heat.shape, F32),
            pltpu.SemaphoreType.DMA((cols + 1,)),
            pltpu.SemaphoreType.DMA((6,)),
            pltpu.SemaphoreType.DMA((SUBS, 4)),
            pltpu.SemaphoreType.DMA((SUBS, 4)),
            pltpu.SemaphoreType.DMA((4,)),
            pltpu.SemaphoreType.DMA((cols,)),
        ],
        compiler_params=pltpu.CompilerParams(
            collective_id=0, has_side_effects=True, vmem_limit_bytes=60 * 1024 * 1024
        ),
    )(level_set, fuel, wind, owner, active.reshape(SUBS), fuel_rate, fuel_wind, fuel_heat)

    return pl.pallas_call(
        hand_out,
        out_shape=(jax.ShapeDtypeStruct(level_set.shape, F32), jax.ShapeDtypeStruct(wind.shape, F32)),
        in_specs=[anywhere] * 2,
        out_specs=(anywhere, anywhere),
        scratch_shapes=[
            pltpu.VMEM(level_set.shape, F32), pltpu.VMEM(wind.shape, F32),
            pltpu.SemaphoreType.DMA((PARTS + 1,)), pltpu.SemaphoreType.DMA((PARTS + 1,)),
        ],
        compiler_params=pltpu.CompilerParams(vmem_limit_bytes=60 * 1024 * 1024),
    )(level, held)


def solution(mesh):
    in_specs = (
        P("grp", "tile"),
        P("grp", "tile"),
        P(None, "grp", "tile"),
        P("grp", None),
        P(None, "grp", "tile"),
        P(),
        P(),
        P(),
    )
    out_specs = (P("grp", "tile"), P(None, "grp", "tile"))
    body = functools.partial(shards, mesh.shape["grp"], mesh.shape["tile"])
    return jax.shard_map(body, mesh=mesh, in_specs=in_specs, out_specs=out_specs, check_vma=False)
```
